128 devices in a mesh: batch: 4 (over z_hi, core), hidden: 32 (over z_lo, y, x).
Axes of the slice: x: 4, y: 4, z: 4 (z_hi: 2, z_lo: 2; z = z_hi * 2 + z_lo), core: 2. Of those that a mesh axis runs over, the one named last changes fastest.
Arguments:
- codes: bfloat16 [640, 9216], P('batch', 'hidden'), may hold values from -6 to 6
- exponents: int32 [640], P('batch'), may hold values from -2 to 2
- w_in: bfloat16 [9216, 36864], P('batch', 'hidden'), may hold values from -0.0625 to 0.0625
- w_out: bfloat16 [36864, 9216], P('hidden', 'batch'), may hold values from -0.0625 to 0.0625
Outputs:
- mixed: float32 [640, 9216], P(None, ('batch', 'hidden'))
The draws below stay inside these ranges and needn't reach their ends.
All inputs are finite; a program needn't handle non-finite values.
Results may differ from the reference program's by a relative error of at most 0.0029.
Values may be sent and summed in bfloat16 or wider, within the bound.
No kernel may reach another device: no remote copies, remote signals or barrier semaphores. Data moves between devices by JAX's collectives and lax.ppermute only.
A program may use at most 128 MiB of HBM per device.

```python
import jax
import jax.numpy as jnp

D = 9216
FF = 36864
TOKENS = 640


def plant(array, own_key, low, high):
    extent = array.shape
    spot = [jax.random.randint(jax.random.fold_in(own_key, axis), (), 0, extent[axis]) for axis in range(len(extent))]
    array = array.at[tuple(spot)].set(low)
    longest = extent.index(max(extent))
    spot[longest] = (spot[longest] + 1) % extent[longest]
    return array.at[tuple(spot)].set(high)


def with_spikes(drawn, own_key, source, target, blocks, factor):
    def block_of(dim):
        return (jnp.arange(drawn.shape[dim]) // (drawn.shape[dim] // blocks)).reshape((-1,) + (1,) * (drawn.ndim - 1 - dim))

    near = jax.random.permutation(own_key, blocks)[block_of(target)]
    other_side = (block_of(target) + blocks // 2) % blocks
    return jnp.where((block_of(source) == near) | (block_of(source) == other_side), factor * drawn, drawn)


def block_scale(own_key, dims, shards, low, largest):
    factor_of, own = 1.0, jax.random.fold_in(own_key, 6)
    for dim, blocks in shards:
        heights = jnp.exp(jax.random.uniform(jax.random.fold_in(own, dim), (blocks,), jnp.float32, low / len(shards), largest / len(shards)))
        factor_of = factor_of * jnp.repeat(heights, dims[dim] // blocks).reshape([-1 if axis == dim else 1 for axis in range(len(dims))])
    return factor_of


def gaussian(key, shape, width, most, shards=(), dtype=jnp.bfloat16):
    array = jax.random.normal(key, shape, jnp.float32) * width
    if len(shards) > 0:
        array = block_scale(key, shape, shards, -0.22, 0.18) * array
    return jnp.clip(array, min=-most, max=most).astype(dtype)


def bell_draw_with(stream_key, extent, deviation, reach, pieces, heavy, kind=jnp.bfloat16):
    values = deviation * jax.random.normal(stream_key, extent, jnp.float32)
    if pieces:
        values = values * block_scale(stream_key, extent, pieces, -0.22, 0.18)
    return jnp.clip(with_spikes(values, jax.random.fold_in(stream_key, 3), *heavy), -reach, reach).astype(kind)


def setup_inputs(seed: int = 0) -> dict:
    keys = jax.random.split(jax.random.key(seed), 5)
    codes = gaussian(keys[0], (TOKENS, D), 1.0, 6.0, ((0, 4), (1, 32)))
    exponents = plant(jax.random.randint(keys[1], (TOKENS,), -2, 3), jax.random.fold_in(keys[1], 1), -2, 2).astype(jnp.int32)
    w_in = gaussian(keys[2], (D, FF), D ** -0.5, 0.0625, ((0, 4), (1, 32)))
    w_out = bell_draw_with(keys[3], (FF, D), FF ** -0.5, 0.0625, ((0, 32), (1, 4)), (0, 1, 32, 2.75))
    return dict(codes=codes, exponents=exponents, w_in=w_in, w_out=w_out)


def reference(codes, exponents, w_in, w_out):
    preact = jnp.dot(codes, w_in, preferred_element_type=jnp.float32)
    preact = preact * jnp.exp2(exponents.astype(jnp.float32))[:, None]
    activ = jax.nn.gelu(preact, approximate=True).astype(jnp.bfloat16)
    return jnp.dot(activ, w_out, preferred_element_type=jnp.float32)
```

```python
import jax
import jax.numpy as jnp
from jax import lax
from jax.experimental import pallas as pl
from jax.experimental.pallas import tpu as pltpu
from jax.sharding import Mesh, PartitionSpec as P

BF, F32 = jnp.bfloat16, jnp.float32
QT = 160
PIECE = 288
UNITS = 1152
CHIP_COLS = 72
VMEM = pl.BlockSpec(memory_space=pltpu.VMEM)
ANY = pl.BlockSpec(memory_space=pl.ANY)
YX = ("c", "y", "x")


def first_axis(step):
    pairs = []
    for y in range(4):
        for x in range(4):
            pairs.append((y * 4 + x, y * 4 + (x + step) % 4))
            pairs.append((16 + y * 4 + x, 16 + (y + step) % 4 * 4 + x))
    return pairs


def second_axis(step):
    pairs = []
    for y in range(4):
        for x in range(4):
            pairs.append((y * 4 + x, (y + step) % 4 * 4 + x))
            pairs.append((16 + y * 4 + x, 16 + y * 4 + (x + step) % 4))
    return pairs


def call(kernel, outs, ins, scratch=(), flops=0, nbytes=0, name=None):
    return pl.pallas_call(
        kernel,
        out_shape=outs,
        in_specs=ins,
        out_specs=jax.tree.map(lambda _: VMEM, outs),
        scratch_shapes=list(scratch),
        compiler_params=pltpu.CompilerParams(vmem_limit_bytes=50 * 2**20),
        cost_estimate=pl.CostEstimate(flops=flops, bytes_accessed=nbytes, transcendentals=0),
        name=name,
    )


def dot(a, b):
    return jnp.dot(a, b, preferred_element_type=F32)


def pack_codes(x_ref, o_ref):
    o_ref[0:QT] = x_ref[:, 0:128]
    o_ref[QT : 2 * QT] = x_ref[:, 128:256]
    tail = x_ref[:, 256:288]
    src = lax.broadcasted_iota(jnp.int32, (32, 128), 0)
    dst = lax.broadcasted_iota(jnp.int32, (32, 128), 1)
    total = jnp.zeros((40, 128), F32)
    for j in range(4):
        place = jnp.where(dst == src + 32 * j, 1.0, 0.0).astype(BF)
        total += dot(tail, place)[40 * j : 40 * j + 40]
    o_ref[2 * QT : 360] = total.astype(BF)


def merge_codes(a_ref, b_ref, c_ref, d_ref, o_ref):
    pieces = (a_ref, b_ref, c_ref, d_ref)
    src = lax.broadcasted_iota(jnp.int32, (512, 128), 0)
    dst = lax.broadcasted_iota(jnp.int32, (512, 128), 1)
    for q in range(2):
        rows = slice(q * QT, (q + 1) * QT)
        for j, ref in enumerate(pieces):
            o_ref[rows, 256 * j : 256 * j + 128] = ref[q, 0:QT]
            o_ref[rows, 256 * j + 128 : 256 * j + 256] = ref[q, QT : 2 * QT]
        tails = jnp.concatenate([ref[q, 2 * QT : 360] for ref in pieces], axis=1)
        groups = []
        for j in range(4):
            place = (src // 128 == dst // 32) & (src % 128 == 32 * j + dst % 32)
            groups.append(dot(tails, jnp.where(place, 1.0, 0.0).astype(BF)))
        o_ref[rows, 1024:1152] = jnp.concatenate(groups, axis=0).astype(BF)


def own_place():
    c, y, x = lax.axis_index("c"), lax.axis_index("y"), lax.axis_index("x")
    return c, jnp.where(c == 0, x, y), jnp.where(c == 0, y, x)


def project_in(m0, m1, m2, m3, own_ref, other_ref, o_ref, w_ref, sems):
    c, first, second = own_place()
    for i in range(4):
        s = lax.rem(second + 4 - i, 4)
        for j in range(4):
            f = lax.rem(first + 4 - j, 4)
            y, x = jnp.where(c == 0, s, f), jnp.where(c == 0, f, s)
            row = lax.rem(y, 2) * UNITS + x * PIECE
            for ref, here in ((own_ref, lax.div(y, 2) == c), (other_ref, lax.div(y, 2) != c)):

                @pl.when(here)
                def _(ref=ref):
                    for at, to, n in ((0, 256 * j, 256), (256, 1024 + 32 * j, 32)):
                        pltpu.make_async_copy(
                            ref.at[pl.ds(pl.multiple_of(row + at, 32), n)], w_ref.at[i, to : to + n], sems.at[i]
                        ).start()

    for i, m in enumerate((m0, m1, m2, m3)):
        pltpu.make_async_copy(w_ref.at[i], w_ref.at[i], sems.at[i]).wait()
        part = dot(m[...], w_ref[i])
        o_ref[...] = part if i == 0 else o_ref[...] + part


def project_out(a_ref, own_ref, other_ref, o0, o1, o2, o3, w_ref, t_ref, tail_ref, sems):
    copies = []
    for g in range(4):
        src = own_ref if g < 2 else other_ref
        copy = pltpu.make_async_copy(src.at[:, (g % 2) * UNITS : (g % 2 + 1) * UNITS], w_ref.at[g], sems.at[g])
        copy.start()
        copies.append(copy)
    for g in range(4):
        copies[g].wait()
        part = dot(a_ref[...], w_ref[g])
        for q in range(2):
            t_ref[5 * q + g] = part[q * QT : q * QT + 128].T.reshape(16, CHIP_COLS, 128)
            tail_ref[q, 32 * g : 32 * g + 32] = part[q * QT + 128 : (q + 1) * QT]
    for q in range(2):
        t_ref[5 * q + 4] = tail_ref[q].T.reshape(16, CHIP_COLS, 128)
    c, first, _ = own_place()
    for rel, o in enumerate((o0, o1, o2, o3)):
        f = lax.rem(first + rel, 4)
        for s in range(4):
            yx = jnp.where(c == 0, s * 4 + f, f * 4 + s)
            for p in range(5):
                both = jnp.concatenate([t_ref[2 * p, yx], t_ref[2 * p + 1, yx]], axis=0)
                o[s, 144 * p : 144 * p + 144] = both.astype(o.dtype)


def add_first(a, b, c, d, o0, o1, o2, o3):
    _, _, second = own_place()
    for rel, o in enumerate((o0, o1, o2, o3)):
        s = lax.rem(second + rel, 4)
        total = a[s] + b[s].astype(F32) + c[s].astype(F32) + d[s].astype(F32)
        o[...] = total.astype(o.dtype)


def add_second(a, b, c, d, keep, to_zl, to_c, to_czl):
    total = a[...] + b[...].astype(F32) + c[...].astype(F32) + d[...].astype(F32)
    zl = lax.axis_index("zl")
    tiles = total.reshape(10, CHIP_COLS, 128)
    lane = lax.broadcasted_iota(jnp.int32, (CHIP_COLS, 128), 1)

    def share(crel, z):
        g = 2 * crel + z
        tail = jnp.where(lane < 32, pltpu.roll(tiles[4], (128 - 32 * g) % 128, 1), pltpu.roll(tiles[9], (160 - 32 * g) % 128, 1))
        return tiles[g], tiles[5 + g], tail

    for crel, same, swapped in ((0, keep, to_zl), (1, to_c, to_czl)):
        for i, (lo, hi) in enumerate(zip(share(crel, 0), share(crel, 1))):
            same[i] = jnp.where(zl == 0, lo, hi)
            swapped[i] = jnp.where(zl == 0, hi, lo)


def finish(keep, from_zl, from_c, from_czl, o_ref):
    c = lax.axis_index("c")
    for core, a, b in ((c, keep, from_zl), (1 - c, from_c, from_czl)):
        tail = (a[2] + b[2]).T
        for q in range(2):
            row = (2 * q + core) * QT
            o_ref[pl.ds(pl.multiple_of(row, 8), 128)] = (a[q] + b[q]).T
            o_ref[pl.ds(pl.multiple_of(row + 128, 8), 32)] = tail[32 * q : 32 * q + 32]


def shape(dims, dtype):
    return jax.ShapeDtypeStruct(dims, dtype)


def shards(codes, exponents, w_in, w_out):
    zh, zl = lax.axis_index("zh"), lax.axis_index("zl")
    swap = [(0, 1), (1, 0)]
    z = ("zh", "zl")
    w_in_other = lax.ppermute(w_in, "c", swap)
    w_out_other = lax.ppermute(w_out, "c", swap)

    packed = call(pack_codes, shape((360, 128), BF), [VMEM], name="pack_codes")(codes)
    one = lax.ppermute(packed, z, [(0, 1), (1, 2), (2, 0), (3, 3)])
    two = lax.ppermute(packed, z, [(2, 1), (3, 2), (1, 3), (0, 0)])
    piece = jnp.stack([jnp.where(zh == zl, two, one), jnp.where(zh == zl, one, two)])

    around = [lax.ppermute(piece, YX, first_axis(k)) for k in (1, 2, 3)]
    merged = call(merge_codes, shape((2 * QT, UNITS), BF), [VMEM] * 4, name="merge_codes")(piece, *around)
    around = [lax.ppermute(merged, YX, second_axis(k)) for k in (1, 2, 3)]
    preact = call(
        project_in,
        shape((2 * QT, UNITS), F32),
        [VMEM] * 4 + [ANY] * 2,
        [pltpu.VMEM((4, UNITS, UNITS), BF), pltpu.SemaphoreType.DMA((4,))],
        flops=2 * 320 * 4608 * 1152,
        nbytes=4608 * 1152 * 2,
        name="project_in",
    )(merged, *around, w_in, w_in_other)

    most = jnp.max(jnp.abs(preact))
    up = jnp.clip(13.0 - jnp.ceil(jnp.log2(jnp.maximum(most, 1e-30))), -100.0, 100.0)
    sent = (preact * jnp.exp2(up)).astype(jnp.float16)
    got = lax.ppermute(sent, "zh", swap)
    got_up = lax.ppermute(jnp.full((8, 128), up), "zh", swap)[0, 0]
    other_exponents = lax.ppermute(exponents, "zh", swap)
    powers = jnp.stack([jnp.where(zh == 0, exponents, other_exponents), jnp.where(zh == 0, other_exponents, exponents)])
    row_scale = jnp.exp2(powers.reshape(2 * QT).astype(F32))[:, None]
    summed = (preact + got.astype(F32) * jnp.exp2(-got_up)) * row_scale
    activ = jax.nn.gelu(summed, approximate=True).astype(BF)

    part = (4, 720, 128)
    mine, *away = call(
        project_out,
        [shape(part, F32)] + [shape(part, BF)] * 3,
        [VMEM] + [ANY] * 2,
        [
            pltpu.VMEM((4, UNITS, UNITS), BF),
            pltpu.VMEM((10, 16, CHIP_COLS, 128), F32),
            pltpu.VMEM((2, 128, UNITS), F32),
            pltpu.SemaphoreType.DMA((4,)),
        ],
        flops=2 * 320 * 4608 * 1152,
        nbytes=4608 * 1152 * 2,
        name="project_out",
    )(activ, w_out, w_out_other)
    away = [lax.ppermute(v, YX, first_axis(k)) for k, v in zip((1, 2, 3), away)]
    part = (720, 128)
    mine, *away = call(add_first, [shape(part, F32)] + [shape(part, BF)] * 3, [VMEM] * 4, name="add_first")(mine, *away)
    away = [lax.ppermute(v, YX, second_axis(k)) for k, v in zip((1, 2, 3), away)]
    keep, to_zl, to_c, to_czl = call(add_second, [shape((3, CHIP_COLS, 128), F32)] * 4, [VMEM] * 4, name="add_second")(mine, *away)
    from_zl = lax.ppermute(to_zl, "zl", swap)
    from_c = lax.ppermute(to_c, "c", swap)
    from_czl = lax.ppermute(to_czl, ("c", "zl"), [(0, 3), (1, 2), (2, 1), (3, 0)])
    return call(finish, shape((4 * QT, CHIP_COLS), F32), [VMEM] * 4, name="finish")(keep, from_zl, from_c, from_czl)


def solution(mesh):
    split = Mesh(mesh.devices.reshape(2, 2, 2, 4, 4), ("zh", "c", "zl", "y", "x"))
    batch, hidden = ("zh", "c"), ("zl", "y", "x")
    placed = (P(batch, hidden), P(batch), P(batch, hidden), P(hidden, batch))
    return jax.shard_map(shards, mesh=split, in_specs=placed, out_specs=P(None, batch + hidden), check_vma=False)
```

```python
import jax
import jax.numpy as jnp
from jax import lax
from jax.experimental import pallas as pl
from jax.experimental.pallas import tpu as pltpu
from jax.sharding import Mesh, PartitionSpec as P

BF, F32 = jnp.bfloat16, jnp.float32
QT = 160
PIECE = 288
UNITS = 1152
CHIP_COLS = 72
VMEM = pl.BlockSpec(memory_space=pltpu.VMEM)
ANY = pl.BlockSpec(memory_space=pl.ANY)
YX = ("c", "y", "x")
STEPS = (0, 2, 1, 3)


def first_axis(step):
    pairs = []
    for y in range(4):
        for x in range(4):
            pairs.append((y * 4 + x, y * 4 + (x + step) % 4))
            pairs.append((16 + y * 4 + x, 16 + (y + step) % 4 * 4 + x))
    return pairs


def second_axis(step):
    pairs = []
    for y in range(4):
        for x in range(4):
            pairs.append((y * 4 + x, (y + step) % 4 * 4 + x))
            pairs.append((16 + y * 4 + x, 16 + y * 4 + (x + step) % 4))
    return pairs


def call(kernel, outs, ins, scratch=(), flops=0, nbytes=0, vmem=8, name=None):
    return pl.pallas_call(
        kernel,
        out_shape=outs,
        in_specs=ins,
        out_specs=jax.tree.map(lambda _: VMEM, outs),
        scratch_shapes=list(scratch),
        compiler_params=pltpu.CompilerParams(vmem_limit_bytes=vmem * 2**20),
        cost_estimate=pl.CostEstimate(flops=flops, bytes_accessed=nbytes, transcendentals=0),
        name=name,
    )


def dot(a, b):
    return jnp.dot(a, b, preferred_element_type=F32)


def pack_codes(x_ref, o_ref):
    o_ref[0:QT] = x_ref[:, 0:128]
    o_ref[QT : 2 * QT] = x_ref[:, 128:256]
    tail = x_ref[:, 256:288]
    src = lax.broadcasted_iota(jnp.int32, (32, 128), 0)
    dst = lax.broadcasted_iota(jnp.int32, (32, 128), 1)
    total = jnp.zeros((40, 128), F32)
    for j in range(4):
        place = jnp.where(dst == src + 32 * j, 1.0, 0.0).astype(BF)
        total += dot(tail, place)[40 * j : 40 * j + 40]
    o_ref[2 * QT : 360] = total.astype(BF)


def merge_codes(a_ref, b_ref, c_ref, d_ref, *outs):
    pieces = (a_ref, b_ref, c_ref, d_ref)
    src = lax.broadcasted_iota(jnp.int32, (512, 128), 0)
    dst = lax.broadcasted_iota(jnp.int32, (512, 128), 1)
    for q, o_ref in enumerate(outs):
        for j, ref in enumerate(pieces):
            o_ref[:, 256 * j : 256 * j + 128] = ref[q, 0:QT]
            o_ref[:, 256 * j + 128 : 256 * j + 256] = ref[q, QT : 2 * QT]
        tails = jnp.concatenate([ref[q, 2 * QT : 360] for ref in pieces], axis=1)
        groups = []
        for j in range(4):
            place = (src // 128 == dst // 32) & (src % 128 == 32 * j + dst % 32)
            groups.append(dot(tails, jnp.where(place, 1.0, 0.0).astype(BF)))
        o_ref[:, 1024:1152] = jnp.concatenate(groups, axis=0).astype(BF)


def own_place():
    c, y, x = lax.axis_index("c"), lax.axis_index("y"), lax.axis_index("x")
    return c, jnp.where(c == 0, x, y), jnp.where(c == 0, y, x)


def arrange_rows(own_ref, other_ref, w_ref, sem):
    c, first, second = own_place()
    for i in range(4):
        s = lax.rem(second + 4 - STEPS[i], 4)
        for j in range(4):
            f = lax.rem(first + 4 - STEPS[j], 4)
            y, x = jnp.where(c == 0, s, f), jnp.where(c == 0, f, s)
            row = lax.rem(y, 2) * UNITS + x * PIECE
            for ref, here in ((own_ref, lax.div(y, 2) == c), (other_ref, lax.div(y, 2) != c)):

                @pl.when(here)
                def _(ref=ref):
                    for at, to, n in ((0, 256 * j, 256), (256, 1024 + 32 * j, 32)):
                        pltpu.make_async_copy(
                            ref.at[pl.ds(pl.multiple_of(row + at, 32), n)], w_ref.at[pl.ds(i * UNITS + to, n)], sem
                        ).start()

    pltpu.make_async_copy(w_ref, w_ref, sem).wait()


def project_in(m0, m1, m2, m3, w_ref, o_ref, scale_ref, power_ref, x_ref):
    for i, m in enumerate((m0, m1, m2, m3)):
        x_ref[:, i * UNITS : (i + 1) * UNITS] = m[...]
    most = jnp.zeros((QT, 128), F32)
    for n in range(0, UNITS, 256):
        to = min(n + 256, UNITS)
        part = dot(x_ref[...], w_ref[:, n:to])
        o_ref[:, n:to] = part
        for k in range(0, to - n, 128):
            most = jnp.maximum(most, jnp.abs(part[:, k : k + 128]))
    most = jnp.full((8, UNITS), jnp.max(most))
    power = 13.0 - jnp.ceil(jnp.log(jnp.maximum(most, 1e-30)) * 1.4426950408889634)
    power_ref[...] = power
    scale_ref[...] = jnp.exp2(power)


def project_out(a_ref, own_ref, other_ref, o0, o1, o2, o3, t_ref, tail_ref):
    for g in range(4):
        w_ref = own_ref if g < 2 else other_ref
        for n in range(0, UNITS, 256):
            to = min(n + 256, UNITS)
            part = dot(a_ref[...], w_ref[:, g % 2 * UNITS + n : g % 2 * UNITS + to])
            t_ref[g, n:to] = part[:128].T
            tail_ref[32 * g : 32 * g + 32, n:to] = part[128:]
    t_ref[4] = tail_ref[...].T
    c, first, _ = own_place()
    for rel, o in zip((0,) + STEPS[1:], (o0, o1, o2, o3)):
        f = lax.rem(first + rel, 4)
        for s in range(4):
            at = pl.ds(pl.multiple_of(jnp.where(c == 0, s * 4 + f, f * 4 + s) * CHIP_COLS, 8), CHIP_COLS)
            for p in range(2):
                both = jnp.concatenate([t_ref[2 * p, at], t_ref[2 * p + 1, at]], axis=0)
                o[s, 144 * p : 144 * p + 144] = both.astype(o.dtype)
            o[s, 288:360] = t_ref[4, at].astype(o.dtype)


def add_first(a0, b0, c0, d0, a1, b1, c1, d1, o0, o1, o2, o3):
    _, _, second = own_place()
    for rel, o in zip(STEPS, (o0, o1, o2, o3)):
        s = lax.rem(second + rel, 4)
        total = [
            a[s] + b[s].astype(F32) + c[s].astype(F32) + d[s].astype(F32) for a, b, c, d in ((a0, b0, c0, d0), (a1, b1, c1, d1))
        ]
        o[...] = jnp.concatenate(total, axis=0).astype(o.dtype)


def add_second(a, b, c, d, keep, to_zl, to_c, to_czl):
    total = a[...] + b[...].astype(F32) + c[...].astype(F32) + d[...].astype(F32)
    zl = lax.axis_index("zl")
    tiles = total.reshape(10, CHIP_COLS, 128)
    lane = lax.broadcasted_iota(jnp.int32, (CHIP_COLS, 128), 1)

    def share(crel, z):
        g = 2 * crel + z
        tail = jnp.where(lane < 32, pltpu.roll(tiles[4], (128 - 32 * g) % 128, 1), pltpu.roll(tiles[9], (160 - 32 * g) % 128, 1))
        return tiles[g], tiles[5 + g], tail

    for crel, same, swapped in ((0, keep, to_zl), (1, to_c, to_czl)):
        for i, (lo, hi) in enumerate(zip(share(crel, 0), share(crel, 1))):
            same[i] = jnp.where(zl == 0, lo, hi)
            swapped[i] = jnp.where(zl == 0, hi, lo)


def finish(keep, from_zl, from_c, from_czl, o_ref):
    c = lax.axis_index("c")
    for core, a, b in ((c, keep, from_zl), (1 - c, from_c, from_czl)):
        tail = (a[2] + b[2]).T
        for q in range(2):
            row = (2 * q + core) * QT
            o_ref[pl.ds(pl.multiple_of(row, 8), 128)] = (a[q] + b[q]).T
            o_ref[pl.ds(pl.multiple_of(row + 128, 8), 32)] = tail[32 * q : 32 * q + 32]


def shape(dims, dtype):
    return jax.ShapeDtypeStruct(dims, dtype)


def shards(codes, exponents, w_in, w_out):
    zh, zl = lax.axis_index("zh"), lax.axis_index("zl")
    swap = [(0, 1), (1, 0)]
    z = ("zh", "zl")
    w_in_other = lax.ppermute(w_in, "c", swap)
    w_out_other = lax.ppermute(w_out, "c", swap)

    packed = call(pack_codes, shape((360, 128), BF), [VMEM], name="pack_codes")(codes)
    one = lax.ppermute(packed, z, [(0, 1), (1, 2), (2, 0), (3, 3)])
    two = lax.ppermute(packed, z, [(2, 1), (3, 2), (1, 3), (0, 0)])
    piece = jnp.stack([jnp.where(zh == zl, two, one), jnp.where(zh == zl, one, two)])

    around = [lax.ppermute(piece, YX, first_axis(k)) for k in STEPS[1:]]
    quarter = shape((QT, UNITS), BF)
    merged = call(merge_codes, [quarter] * 2, [VMEM] * 4, name="merge_codes")(piece, *around)
    around = [[lax.ppermute(m, YX, second_axis(k)) for k in STEPS[1:]] for m in merged]
    weights = call(
        arrange_rows,
        shape((4 * UNITS, UNITS), BF),
        [ANY] * 2,
        [pltpu.SemaphoreType.DMA],
        nbytes=2 * 4608 * 1152 * 2,
        name="arrange_rows",
    )(w_in, w_in_other)
    other_exponents = lax.ppermute(exponents, "zh", swap)
    powers = [jnp.where(zh == 0, exponents, other_exponents), jnp.where(zh == 0, other_exponents, exponents)]

    scattered = []
    for m, others, power in zip(merged, around, powers):
        preact, scale, scale_power = call(
            project_in,
            [shape((QT, UNITS), F32)] + [shape((8, UNITS), F32)] * 2,
            [VMEM] * 5,
            [pltpu.VMEM((QT, 4 * UNITS), BF)],
            flops=2 * QT * 4608 * 1152,
            nbytes=4608 * 1152 * 2,
            name="project_in",
        )(m, *others, weights)
        sent = jnp.concatenate([(preact * scale[:1]).astype(jnp.float16), scale_power.astype(jnp.float16)])
        got = lax.ppermute(sent, "zh", swap).astype(F32)
        row_scale = jnp.exp2(power.astype(F32))[:, None]
        summed = (preact + got[:QT] * jnp.exp2(-got[QT : QT + 1])) * row_scale
        activ = jax.nn.gelu(summed, approximate=True).astype(BF)
        part = (4, 360, 128)
        mine, *away = call(
            project_out,
            [shape(part, F32)] + [shape(part, BF)] * 3,
            [VMEM] * 3,
            [pltpu.VMEM((5, UNITS, 128), F32), pltpu.VMEM((128, UNITS), F32)],
            flops=2 * QT * 4608 * 1152,
            nbytes=4608 * 1152 * 2,
            vmem=12,
            name="project_out",
        )(activ, w_out, w_out_other)
        scattered += [mine] + [lax.ppermute(v, YX, first_axis(k)) for k, v in zip(STEPS[1:], away)]
    part = (720, 128)
    mine, *away = call(add_first, [shape(part, F32)] + [shape(part, BF)] * 3, [VMEM] * 8, name="add_first")(*scattered)
    away = [lax.ppermute(v, YX, second_axis(k)) for k, v in zip(STEPS[1:], away)]
    keep, to_zl, to_c, to_czl = call(add_second, [shape((3, CHIP_COLS, 128), F32)] * 4, [VMEM] * 4, name="add_second")(mine, *away)
    from_zl = lax.ppermute(to_zl, "zl", swap)
    from_c = lax.ppermute(to_c, "c", swap)
    from_czl = lax.ppermute(to_czl, ("c", "zl"), [(0, 3), (1, 2), (2, 1), (3, 0)])
    return call(finish, shape((4 * QT, CHIP_COLS), F32), [VMEM] * 4, name="finish")(keep, from_zl, from_c, from_czl)


def solution(mesh):
    split = Mesh(mesh.devices.reshape(2, 2, 2, 4, 4), ("zh", "c", "zl", "y", "x"))
    batch, hidden = ("zh", "c"), ("zl", "y", "x")
    placed = (P(batch, hidden), P(batch), P(batch, hidden), P(hidden, batch))
    return jax.shard_map(shards, mesh=split, in_specs=placed, out_specs=P(None, batch + hidden), check_vma=False)
```

```python
import jax
import jax.numpy as jnp
from jax import lax
from jax.experimental import pallas as pl
from jax.experimental.pallas import tpu as pltpu
from jax.sharding import Mesh, PartitionSpec as P

BF, F32 = jnp.bfloat16, jnp.float32
QT = 160
PIECE = 288
UNITS = 1152
CHIP_COLS = 72
VMEM = pl.BlockSpec(memory_space=pltpu.VMEM)
HBM = pl.BlockSpec(memory_space=pltpu.HBM)
ANY = pl.BlockSpec(memory_space=pl.ANY)
YX = ("c", "y", "x")
STEPS = (0, 2, 1, 3)


def first_axis(step):
    pairs = []
    for y in range(4):
        for x in range(4):
            pairs.append((y * 4 + x, y * 4 + (x + step) % 4))
            pairs.append((16 + y * 4 + x, 16 + (y + step) % 4 * 4 + x))
    return pairs


def second_axis(step):
    pairs = []
    for y in range(4):
        for x in range(4):
            pairs.append((y * 4 + x, (y + step) % 4 * 4 + x))
            pairs.append((16 + y * 4 + x, 16 + y * 4 + (x + step) % 4))
    return pairs


def call(kernel, outs, ins, scratch=(), flops=0, nbytes=0, vmem=8, name=None):
    return pl.pallas_call(
        kernel,
        out_shape=outs,
        in_specs=ins,
        out_specs=jax.tree.map(lambda _: VMEM, outs),
        scratch_shapes=list(scratch),
        compiler_params=pltpu.CompilerParams(vmem_limit_bytes=vmem * 2**20),
        cost_estimate=pl.CostEstimate(flops=flops, bytes_accessed=nbytes, transcendentals=0),
        name=name,
    )


def dot(a, b):
    return jnp.dot(a, b, preferred_element_type=F32)


def pack_codes(x_ref, e_ref, o_ref):
    row = lax.broadcasted_iota(jnp.int32, (QT, QT), 0)
    col = lax.broadcasted_iota(jnp.int32, (QT, QT), 1)
    power = jnp.exp2(jnp.broadcast_to(e_ref[...], (QT, QT)).astype(F32))
    scale = jnp.where(row == col, power, 0.0).astype(BF)
    x = dot(scale, x_ref[...]).astype(BF)
    o_ref[0:QT] = x[:, 0:128]
    o_ref[QT : 2 * QT] = x[:, 128:256]
    tail = x[:, 256:288]
    src = lax.broadcasted_iota(jnp.int32, (32, 128), 0)
    dst = lax.broadcasted_iota(jnp.int32, (32, 128), 1)
    total = jnp.zeros((40, 128), F32)
    for j in range(4):
        place = jnp.where(dst == src + 32 * j, 1.0, 0.0).astype(BF)
        total += dot(tail, place)[40 * j : 40 * j + 40]
    o_ref[2 * QT : 360] = total.astype(BF)


def merge_codes(a_ref, b_ref, c_ref, d_ref, after1, after2, *outs):
    del after1, after2
    pieces = (a_ref, b_ref, c_ref, d_ref)
    src = lax.broadcasted_iota(jnp.int32, (512, 128), 0)
    dst = lax.broadcasted_iota(jnp.int32, (512, 128), 1)
    for q, o_ref in enumerate(outs):
        for j, ref in enumerate(pieces):
            o_ref[:, 256 * j : 256 * j + 128] = ref[q, 0:QT]
            o_ref[:, 256 * j + 128 : 256 * j + 256] = ref[q, QT : 2 * QT]
        tails = jnp.concatenate([ref[q, 2 * QT : 360] for ref in pieces], axis=1)
        groups = []
        for j in range(4):
            place = (src // 128 == dst // 32) & (src % 128 == 32 * j + dst % 32)
            groups.append(dot(tails, jnp.where(place, 1.0, 0.0).astype(BF)))
        o_ref[:, 1024:1152] = jnp.concatenate(groups, axis=0).astype(BF)


def own_place():
    c, y, x = lax.axis_index("c"), lax.axis_index("y"), lax.axis_index("x")
    return c, jnp.where(c == 0, x, y), jnp.where(c == 0, y, x)


def arrange_rows(own_ref, other_ref, w_ref, sem):
    c, first, second = own_place()
    for i in range(4):
        s = lax.rem(second + 4 - STEPS[i], 4)
        for j in range(4):
            f = lax.rem(first + 4 - STEPS[j], 4)
            y, x = jnp.where(c == 0, s, f), jnp.where(c == 0, f, s)
            row = lax.rem(y, 2) * UNITS + x * PIECE
            for ref, here in ((own_ref, lax.div(y, 2) == c), (other_ref, lax.div(y, 2) != c)):

                @pl.when(here)
                def _(ref=ref):
                    for at, to, n in ((0, 256 * j, 256), (256, 1024 + 32 * j, 32)):
                        pltpu.make_async_copy(
                            ref.at[pl.ds(pl.multiple_of(row + at, 32), n)], w_ref.at[pl.ds(i * UNITS + to, n)], sem
                        ).start()

    pltpu.make_async_copy(w_ref, w_ref, sem).wait()


def stage_columns(own_ref, other_ref, after, w_ref, sem):
    del after
    for ref, at in ((own_ref, 0), (other_ref, 2 * UNITS)):
        pltpu.make_async_copy(ref, w_ref.at[:, at : at + 2 * UNITS], sem).start()
    pltpu.make_async_copy(w_ref, w_ref, sem).wait()


def project_in(m0, m1, m2, m3, w_ref, o_ref, send_ref, x_ref):
    for i, m in enumerate((m0, m1, m2, m3)):
        x_ref[:, i * UNITS : (i + 1) * UNITS] = m[...]
    most = jnp.zeros((QT, 128), F32)
    for n in range(0, UNITS, 256):
        to = min(n + 256, UNITS)
        part = dot(x_ref[...], w_ref[:, n:to])
        o_ref[:, n:to] = part
        for k in range(0, to - n, 128):
            most = jnp.maximum(most, jnp.abs(part[:, k : k + 128]))
    most = jnp.full((8, UNITS), jnp.max(most))
    power = 13.0 - jnp.ceil(jnp.log(jnp.maximum(most, 1e-30)) * 1.4426950408889634)
    send_ref[0:QT] = o_ref[...] * jnp.exp2(power)[:1]
    send_ref[QT:] = power


def project_out(a_ref, w_ref, o0, o1, o2, o3, t_ref, tail_ref):
    for g in range(4):
        for n in range(0, UNITS, 256):
            to = min(n + 256, UNITS)
            part = dot(a_ref[...], w_ref[:, g * UNITS + n : g * UNITS + to])
            t_ref[g, n:to] = part[:128].T
            tail_ref[32 * g : 32 * g + 32, n:to] = part[128:]
    t_ref[4] = tail_ref[...].T
    c, first, _ = own_place()
    for rel, o in zip(STEPS, (o0, o1, o2, o3)):
        f = lax.rem(first + rel, 4)
        for s in range(4):
            at = pl.ds(pl.multiple_of(jnp.where(c == 0, s * 4 + f, f * 4 + s) * CHIP_COLS, 8), CHIP_COLS)
            for p in range(2):
                both = jnp.concatenate([t_ref[2 * p, at], t_ref[2 * p + 1, at]], axis=0)
                o[s, 144 * p : 144 * p + 144] = both.astype(o.dtype)
            o[s, 288:360] = t_ref[4, at].astype(o.dtype)


def add_first(a0, b0, c0, d0, a1, b1, c1, d1, o0, o1, o2, o3):
    _, _, second = own_place()
    for rel, o in zip(STEPS, (o0, o1, o2, o3)):
        s = lax.rem(second + rel, 4)
        total = [
            a[s] + b[s].astype(F32) + c[s].astype(F32) + d[s].astype(F32) for a, b, c, d in ((a0, b0, c0, d0), (a1, b1, c1, d1))
        ]
        o[...] = jnp.concatenate(total, axis=0).astype(o.dtype)


def add_second(a, b, c, d, keep, to_zl, to_c, to_czl):
    total = a[...] + b[...].astype(F32) + c[...].astype(F32) + d[...].astype(F32)
    zl = lax.axis_index("zl")
    tiles = total.reshape(10, CHIP_COLS, 128)
    lane = lax.broadcasted_iota(jnp.int32, (CHIP_COLS, 128), 1)

    def share(crel, z):
        g = 2 * crel + z
        tail = jnp.where(lane < 32, pltpu.roll(tiles[4], (128 - 32 * g) % 128, 1), pltpu.roll(tiles[9], (160 - 32 * g) % 128, 1))
        return tiles[g], tiles[5 + g], tail

    for crel, same, swapped in ((0, keep, to_zl), (1, to_c, to_czl)):
        for i, (lo, hi) in enumerate(zip(share(crel, 0), share(crel, 1))):
            same[i] = jnp.where(zl == 0, lo, hi)
            swapped[i] = jnp.where(zl == 0, hi, lo)


def finish(keep, from_zl, from_c, from_czl, o_ref):
    c = lax.axis_index("c")
    for core, a, b in ((c, keep, from_zl), (1 - c, from_c, from_czl)):
        tail = (a[2] + b[2]).T
        for q in range(2):
            row = (2 * q + core) * QT
            o_ref[pl.ds(pl.multiple_of(row, 8), 128)] = (a[q] + b[q]).T
            o_ref[pl.ds(pl.multiple_of(row + 128, 8), 32)] = tail[32 * q : 32 * q + 32]


def shape(dims, dtype):
    return jax.ShapeDtypeStruct(dims, dtype)


def shards(codes, exponents, w_in, w_out):
    zh, zl = lax.axis_index("zh"), lax.axis_index("zl")
    swap = [(0, 1), (1, 0)]
    z = ("zh", "zl")
    w_in_other = lax.ppermute(w_in, "c", swap)
    w_out_other = lax.ppermute(w_out, "c", swap)
    w_in, w_out = (pltpu.with_memory_space_constraint(w, pltpu.HBM) for w in (w_in, w_out))

    packed = call(pack_codes, shape((360, 128), BF), [VMEM] * 2, name="pack_codes")(codes, exponents[None, :])
    one = lax.ppermute(packed, z, [(0, 1), (1, 2), (2, 0), (3, 3)])
    two = lax.ppermute(packed, z, [(2, 1), (3, 2), (1, 3), (0, 0)])
    piece = jnp.stack([jnp.where(zh == zl, two, one), jnp.where(zh == zl, one, two)])

    around = [lax.ppermute(piece, YX, first_axis(k)) for k in STEPS[1:]]
    weights = call(
        arrange_rows,
        pltpu.VMEM((4 * UNITS, UNITS), BF),
        [HBM, ANY],
        [pltpu.SemaphoreType.DMA],
        nbytes=2 * 4608 * 1152 * 2,
        vmem=8,
        name="arrange_rows",
    )(w_in, w_in_other)
    quarter = shape((QT, UNITS), BF)
    merged = call(merge_codes, [quarter] * 2, [VMEM] * 4 + [ANY] * 2, name="merge_codes")(piece, *around, weights, w_out_other)
    around = [[lax.ppermute(m, YX, second_axis(k)) for k in STEPS[1:]] for m in merged]

    preacts, sends = [], []
    for q in range(2):
        preact, send = call(
            project_in,
            [shape((QT, UNITS), F32), shape((QT + 8, UNITS), F32)],
            [VMEM] * 5,
            [pltpu.VMEM((QT, 4 * UNITS), BF)],
            flops=2 * QT * 4608 * 1152,
            nbytes=4608 * 1152 * 2,
            name="project_in",
        )(merged[q], *around[q], weights)
        preacts.append(preact)
        sends.append(send.astype(jnp.float16))
    gots = [lax.ppermute(send, "zh", swap) for send in sends]
    weights = call(
        stage_columns,
        pltpu.VMEM((UNITS, 4 * UNITS), BF),
        [HBM, ANY, ANY],
        [pltpu.SemaphoreType.DMA],
        nbytes=2 * 4608 * 1152 * 2,
        vmem=8,
        name="stage_columns",
    )(w_out, w_out_other, preacts[1])

    scattered = []
    for preact, got in zip(preacts, gots):
        other = got[:QT].astype(F32) * jnp.exp2(-got[QT : QT + 1].astype(F32))
        activ = jax.nn.gelu(preact + other, approximate=True).astype(BF)
        part = (4, 360, 128)
        mine, *away = call(
            project_out,
            [shape(part, F32)] + [shape(part, BF)] * 3,
            [VMEM] * 2,
            [pltpu.VMEM((5, UNITS, 128), F32), pltpu.VMEM((128, UNITS), F32)],
            flops=2 * QT * 4608 * 1152,
            nbytes=4608 * 1152 * 2,
            vmem=12,
            name="project_out",
        )(activ, weights)
        scattered += [mine] + [lax.ppermute(v, YX, first_axis(k)) for k, v in zip(STEPS[1:], away)]
    part = (720, 128)
    mine, *away = call(add_first, [shape(part, F32)] + [shape(part, BF)] * 3, [VMEM] * 8, name="add_first")(*scattered)
    away = [lax.ppermute(v, YX, second_axis(k)) for k, v in zip(STEPS[1:], away)]
    keep, to_zl, to_c, to_czl = call(add_second, [shape((3, CHIP_COLS, 128), F32)] * 4, [VMEM] * 4, name="add_second")(mine, *away)
    from_zl = lax.ppermute(to_zl, "zl", swap)
    from_c = lax.ppermute(to_c, "c", swap)
    from_czl = lax.ppermute(to_czl, ("c", "zl"), [(0, 3), (1, 2), (2, 1), (3, 0)])
    return call(finish, shape((4 * QT, CHIP_COLS), F32), [VMEM] * 4, name="finish")(keep, from_zl, from_c, from_czl)


def solution(mesh):
    split = Mesh(mesh.devices.reshape(2, 2, 2, 4, 4), ("zh", "c", "zl", "y", "x"))
    batch, hidden = ("zh", "c"), ("zl", "y", "x")
    placed = (P(batch, hidden), P(batch), P(batch, hidden), P(hidden, batch))
    return jax.shard_map(shards, mesh=split, in_specs=placed, out_specs=P(None, batch + hidden), check_vma=False)
```

```python
import jax
import jax.numpy as jnp
from jax import lax
from jax.experimental import pallas as pl
from jax.experimental.pallas import tpu as pltpu
from jax.sharding import Mesh, PartitionSpec as P

BF, F32 = jnp.bfloat16, jnp.float32
QT = 160
PIECE = 288
UNITS = 1152
CHIP_COLS = 72
VMEM = pl.BlockSpec(memory_space=pltpu.VMEM)
ANY = pl.BlockSpec(memory_space=pl.ANY)
YX = ("c", "y", "x")
STEPS = (0, 2, 1, 3)
GATHER = (0, 3, 1, 2)


def first_axis(step):
    pairs = []
    for y in range(4):
        for x in range(4):
            pairs.append((y * 4 + x, y * 4 + (x + step) % 4))
            pairs.append((16 + y * 4 + x, 16 + (y + step) % 4 * 4 + x))
    return pairs


def second_axis(step):
    pairs = []
    for y in range(4):
        for x in range(4):
            pairs.append((y * 4 + x, (y + step) % 4 * 4 + x))
            pairs.append((16 + y * 4 + x, 16 + y * 4 + (x + step) % 4))
    return pairs


def call(kernel, outs, ins, scratch=(), flops=0, nbytes=0, vmem=8, alias={}, name=None):
    return pl.pallas_call(
        kernel,
        out_shape=outs,
        in_specs=ins,
        out_specs=jax.tree.map(lambda _: VMEM, outs),
        input_output_aliases=alias,
        scratch_shapes=list(scratch),
        compiler_params=pltpu.CompilerParams(vmem_limit_bytes=vmem * 2**20),
        cost_estimate=pl.CostEstimate(flops=flops, bytes_accessed=nbytes, transcendentals=0),
        name=name,
    )


def dot(a, b):
    return jnp.dot(a, b, preferred_element_type=F32)


def pack_codes(codes_ref, exponents_ref, o_ref, x_ref, e_ref, sems):
    copies = [
        pltpu.make_async_copy(codes_ref, x_ref, sems.at[0]),
        pltpu.make_async_copy(exponents_ref, e_ref, sems.at[1]),
    ]
    for copy in copies:
        copy.start()
    row = lax.broadcasted_iota(jnp.int32, (QT, QT), 0)
    col = lax.broadcasted_iota(jnp.int32, (QT, QT), 1)
    for copy in copies:
        copy.wait()
    power = jnp.exp2(jnp.broadcast_to(e_ref[...], (QT, QT)).astype(F32))
    scale = jnp.where(row == col, power, 0.0).astype(BF)
    x = dot(scale, x_ref[...]).astype(BF)
    o_ref[0:QT] = x[:, 0:128]
    o_ref[QT : 2 * QT] = x[:, 128:256]
    tail = x[:, 256:288]
    src = lax.broadcasted_iota(jnp.int32, (32, 128), 0)
    dst = lax.broadcasted_iota(jnp.int32, (32, 128), 1)
    total = jnp.zeros((40, 128), F32)
    for j in range(4):
        place = jnp.where(dst == src + 32 * j, 1.0, 0.0).astype(BF)
        total += dot(tail, place)[40 * j : 40 * j + 40]
    o_ref[2 * QT : 360] = total.astype(BF)


def order_quarters(one, two, after, o_ref):
    del after
    same = lax.axis_index("zh") == lax.axis_index("zl")
    o_ref[0] = jnp.where(same, two[...], one[...])
    o_ref[1] = jnp.where(same, one[...], two[...])


def merge_codes(a_ref, b_ref, c_ref, d_ref, after1, after2, *outs):
    del after1, after2
    pieces = (a_ref, b_ref, c_ref, d_ref)
    src = lax.broadcasted_iota(jnp.int32, (512, 128), 0)
    dst = lax.broadcasted_iota(jnp.int32, (512, 128), 1)
    for q, o_ref in enumerate(outs):
        for j, ref in enumerate(pieces):
            o_ref[:, 256 * j : 256 * j + 128] = ref[q, 0:QT]
            o_ref[:, 256 * j + 128 : 256 * j + 256] = ref[q, QT : 2 * QT]
        tails = jnp.concatenate([ref[q, 2 * QT : 360] for ref in pieces], axis=1)
        groups = []
        for j in range(4):
            place = (src // 128 == dst // 32) & (src % 128 == 32 * j + dst % 32)
            groups.append(dot(tails, jnp.where(place, 1.0, 0.0).astype(BF)))
        o_ref[:, 1024:1152] = jnp.concatenate(groups, axis=0).astype(BF)


def own_place():
    c, y, x = lax.axis_index("c"), lax.axis_index("y"), lax.axis_index("x")
    return c, jnp.where(c == 0, x, y), jnp.where(c == 0, y, x)


def arrange_rows(own, ref, w_ref, sem):
    c, first, second = own_place()
    for i in range(4):
        s = lax.rem(second + 4 - GATHER[i], 4)
        for j in range(4):
            f = lax.rem(first + 4 - GATHER[j], 4)
            y, x = jnp.where(c == 0, s, f), jnp.where(c == 0, f, s)
            row = lax.rem(y, 2) * UNITS + x * PIECE

            @pl.when((lax.div(y, 2) == c) == own)
            def _():
                for at, to, n in ((0, 256 * j, 256), (256, 1024 + 32 * j, 32)):
                    pltpu.make_async_copy(
                        ref.at[pl.ds(pl.multiple_of(row + at, 32), n)], w_ref.at[pl.ds(i * UNITS + to, n)], sem
                    ).start()

    pltpu.make_async_copy(w_ref.at[: 2 * UNITS], w_ref.at[: 2 * UNITS], sem).wait()


def arrange_own(ref, w_ref, sem):
    arrange_rows(True, ref, w_ref, sem)


def arrange_other(ref, half_ref, w_ref, sem):
    del half_ref
    arrange_rows(False, ref, w_ref, sem)


def stage_own(ref, after, w_ref, sem):
    del after
    copy = pltpu.make_async_copy(ref, w_ref.at[:, : 2 * UNITS], sem)
    copy.start()
    copy.wait()


def stage_other(ref, half_ref, w_ref, sem):
    del half_ref
    copy = pltpu.make_async_copy(ref, w_ref.at[:, 2 * UNITS :], sem)
    copy.start()
    copy.wait()


def scaled(x):
    most = jnp.full((8, x.shape[1]), jnp.max(jnp.abs(x)))
    power = 13.0 - jnp.ceil(jnp.log(jnp.maximum(most, 1e-30)) * 1.4426950408889634)
    return x * jnp.exp2(power)[:1], power


def project_in(m0, m1, m2, m3, w_ref, o_ref, send_ref, x_ref):
    for i, m in enumerate((m0, m1, m2, m3)):
        x_ref[:, i * UNITS : (i + 1) * UNITS] = m[...]
    for n in range(0, UNITS, 256):
        to = min(n + 256, UNITS)
        o_ref[:, n:to] = dot(x_ref[...], w_ref[:, n:to])
    send_ref[0:QT], send_ref[QT:] = scaled(o_ref[...])


def project_out(a_ref, w_ref, o0, o1, o2, o3, t_ref, tail_ref):
    for g in range(4):
        for n in range(0, UNITS, 256):
            to = min(n + 256, UNITS)
            part = dot(a_ref[...], w_ref[:, g * UNITS + n : g * UNITS + to])
            t_ref[g, n:to] = part[:128].T
            tail_ref[32 * g : 32 * g + 32, n:to] = part[128:]
    t_ref[4] = tail_ref[...].T
    c, first, _ = own_place()
    for rel, o in zip(STEPS, (o0, o1, o2, o3)):
        f = lax.rem(first + rel, 4)
        for s in range(4):
            at = pl.ds(pl.multiple_of(jnp.where(c == 0, s * 4 + f, f * 4 + s) * CHIP_COLS, 8), CHIP_COLS)
            for p in range(2):
                both = jnp.concatenate([t_ref[2 * p, at], t_ref[2 * p + 1, at]], axis=0)
                o[s, 144 * p : 144 * p + 144] = both.astype(o.dtype)
            o[s, 288:360] = t_ref[4, at].astype(o.dtype)


def add_first(a0, b0, c0, d0, a1, b1, c1, d1, o0, o1, o2, o3):
    _, _, second = own_place()
    for rel, o in zip(STEPS, (o0, o1, o2, o3)):
        s = lax.rem(second + rel, 4)
        total = [
            a[s] + b[s].astype(F32) + c[s].astype(F32) + d[s].astype(F32) for a, b, c, d in ((a0, b0, c0, d0), (a1, b1, c1, d1))
        ]
        o[...] = jnp.concatenate(total, axis=0).astype(o.dtype)


def add_second(a, b, c, d, keep, to_zl, to_c, to_czl):
    total = a[...] + b[...].astype(F32) + c[...].astype(F32) + d[...].astype(F32)
    zl = lax.axis_index("zl")
    tiles = total.reshape(10, CHIP_COLS, 128)
    lane = lax.broadcasted_iota(jnp.int32, (CHIP_COLS, 128), 1)

    def share(crel, z):
        g = 2 * crel + z
        tail = jnp.where(lane < 32, pltpu.roll(tiles[4], (128 - 32 * g) % 128, 1), pltpu.roll(tiles[9], (160 - 32 * g) % 128, 1))
        return tiles[g], tiles[5 + g], tail

    shares = []
    for crel in range(2):
        lo, hi = (jnp.concatenate(share(crel, z), axis=0) for z in range(2))
        shares.append((jnp.where(zl == 0, lo, hi), jnp.where(zl == 0, hi, lo)))
    keep[...] = shares[0][0]
    to_c[...] = shares[1][0]
    for ref, (_, value) in zip((to_zl, to_czl), shares):
        ref[0:216], ref[216:] = scaled(value)


def finish(keep, from_zl, from_c, from_czl, o_ref):
    c = lax.axis_index("c")
    for core, a, b in ((c, keep, from_zl), (1 - c, from_c, from_czl)):
        total = a[...] + b[0:216] * jnp.exp2(-b[216:])[:1]
        tail = total[144:].T
        for q in range(2):
            row = (2 * q + core) * QT
            o_ref[pl.ds(pl.multiple_of(row, 8), 128)] = total[72 * q : 72 * q + 72].T
            o_ref[pl.ds(pl.multiple_of(row + 128, 8), 32)] = tail[32 * q : 32 * q + 32]


def shape(dims, dtype):
    return jax.ShapeDtypeStruct(dims, dtype)


def in_hbm(x):
    return pltpu.with_memory_space_constraint(x, pltpu.HBM)


def shards(codes, exponents, w_in, w_out):
    zh, zl = lax.axis_index("zh"), lax.axis_index("zl")
    swap = [(0, 1), (1, 0)]
    z = ("zh", "zl")
    w_in_other = lax.ppermute(w_in, "c", swap)
    w_out_other = lax.ppermute(w_out, "c", swap)
    w_in, w_out = in_hbm(w_in), in_hbm(w_out)

    packed = call(
        pack_codes,
        shape((360, 128), BF),
        [ANY] * 2,
        [pltpu.VMEM((QT, PIECE), BF), pltpu.VMEM((1, QT), jnp.int32), pltpu.SemaphoreType.DMA((2,))],
        name="pack_codes",
    )(in_hbm(codes), in_hbm(exponents[None, :]))
    one = lax.ppermute(packed, z, [(0, 1), (1, 2), (2, 0), (3, 3)])
    two = lax.ppermute(packed, z, [(2, 1), (3, 2), (1, 3), (0, 0)])
    dma, half = [pltpu.SemaphoreType.DMA], 4608 * 1152 * 2
    rows = call(arrange_own, pltpu.VMEM((4 * UNITS, UNITS), BF), [ANY], dma, nbytes=half, name="arrange_own")(w_in)
    piece = call(order_quarters, shape((2, 360, 128), BF), [VMEM, VMEM, ANY], name="order_quarters")(one, two, rows)
    around = [lax.ppermute(piece, YX, first_axis(k)) for k in GATHER[1:]]
    rows = call(
        arrange_other, pltpu.VMEM((4 * UNITS, UNITS), BF), [ANY, VMEM], dma, nbytes=half, alias={1: 0}, name="arrange_other"
    )(w_in_other, rows)
    quarter = shape((QT, UNITS), BF)
    merged = call(merge_codes, [quarter] * 2, [VMEM] * 4 + [ANY] * 2, name="merge_codes")(piece, *around, rows, w_out_other)
    around = [[lax.ppermute(m, YX, second_axis(k)) for k in GATHER[1:]] for m in merged]

    preacts, sends = [], []
    for q in range(2):
        preact, send = call(
            project_in,
            [shape((QT, UNITS), F32), shape((QT + 8, UNITS), F32)],
            [VMEM] * 5,
            [pltpu.VMEM((QT, 4 * UNITS), BF)],
            flops=2 * QT * 4608 * 1152,
            nbytes=4608 * 1152 * 2,
            name="project_in",
        )(merged[q], *around[q], rows)
        preacts.append(preact)
        sends.append(send.astype(jnp.float16))
    gots = [lax.ppermute(send, "zh", swap) for send in sends]
    columns = call(stage_own, pltpu.VMEM((UNITS, 4 * UNITS), BF), [ANY] * 2, dma, nbytes=half, name="stage_own")(w_out, merged[0])
    columns = call(
        stage_other, pltpu.VMEM((UNITS, 4 * UNITS), BF), [ANY, VMEM], dma, nbytes=half, alias={1: 0}, name="stage_other"
    )(w_out_other, columns)

    scattered = []
    for preact, got in zip(preacts, gots):
        other = got[:QT].astype(F32) * jnp.exp2(-got[QT : QT + 1].astype(F32))
        activ = jax.nn.gelu(preact + other, approximate=True).astype(BF)
        part = (4, 360, 128)
        mine, *away = call(
            project_out,
            [shape(part, F32)] + [shape(part, BF)] * 3,
            [VMEM] * 2,
            [pltpu.VMEM((5, UNITS, 128), F32), pltpu.VMEM((128, UNITS), F32)],
            flops=2 * QT * 4608 * 1152,
            nbytes=4608 * 1152 * 2,
            vmem=12,
            name="project_out",
        )(activ, columns)
        scattered += [mine] + [lax.ppermute(v, YX, first_axis(k)) for k, v in zip(STEPS[1:], away)]
    part = (720, 128)
    mine, *away = call(add_first, [shape(part, F32)] + [shape(part, BF)] * 3, [VMEM] * 8, name="add_first")(*scattered)
    away = [lax.ppermute(v, YX, second_axis(k)) for k, v in zip(STEPS[1:], away)]
    plain, with_power = shape((216, 128), F32), shape((224, 128), F32)
    keep, to_zl, to_c, to_czl = call(add_second, [plain, with_power] * 2, [VMEM] * 4, name="add_second")(mine, *away)
    from_zl = lax.ppermute(to_zl.astype(jnp.float16), "zl", swap).astype(F32)
    from_czl = lax.ppermute(to_czl.astype(jnp.float16), ("c", "zl"), [(0, 3), (1, 2), (2, 1), (3, 0)]).astype(F32)
    from_c = lax.ppermute(to_c, "c", swap)
    return call(finish, shape((4 * QT, CHIP_COLS), F32), [VMEM] * 4, name="finish")(keep, from_zl, from_c, from_czl)


def solution(mesh):
    split = Mesh(mesh.devices.reshape(2, 2, 2, 4, 4), ("zh", "c", "zl", "y", "x"))
    batch, hidden = ("zh", "c"), ("zl", "y", "x")
    placed = (P(batch, hidden), P(batch), P(batch, hidden), P(hidden, batch))
    return jax.shard_map(shards, mesh=split, in_specs=placed, out_specs=P(None, batch + hidden), check_vma=False)
```

```python
import jax
import jax.numpy as jnp
from jax import lax
from jax.experimental import pallas as pl
from jax.experimental.pallas import tpu as pltpu
from jax.sharding import Mesh, PartitionSpec as P

BF, F32 = jnp.bfloat16, jnp.float32
QT = 160
PIECE = 288
UNITS = 1152
CHIP_COLS = 72
VMEM = pl.BlockSpec(memory_space=pltpu.VMEM)
ANY = pl.BlockSpec(memory_space=pl.ANY)
YX = ("c", "y", "x")
STEPS = (0, 2, 1, 3)
GATHER = (0, 3, 1, 2)
ARRIVES = (0, 2, 3, 1)


def first_axis(step):
    pairs = []
    for y in range(4):
        for x in range(4):
            pairs.append((y * 4 + x, y * 4 + (x + step) % 4))
            pairs.append((16 + y * 4 + x, 16 + (y + step) % 4 * 4 + x))
    return pairs


def second_axis(step):
    pairs = []
    for y in range(4):
        for x in range(4):
            pairs.append((y * 4 + x, (y + step) % 4 * 4 + x))
            pairs.append((16 + y * 4 + x, 16 + y * 4 + (x + step) % 4))
    return pairs


def call(kernel, outs, ins, scratch=(), flops=0, nbytes=0, vmem=8, alias={}, out_specs=None, name=None):
    return pl.pallas_call(
        kernel,
        out_shape=outs,
        in_specs=ins,
        out_specs=out_specs or jax.tree.map(lambda _: VMEM, outs),
        input_output_aliases=alias,
        scratch_shapes=list(scratch),
        compiler_params=pltpu.CompilerParams(vmem_limit_bytes=vmem * 2**20),
        cost_estimate=pl.CostEstimate(flops=flops, bytes_accessed=nbytes, transcendentals=0),
        name=name,
    )


def dot(a, b):
    return jnp.dot(a, b, preferred_element_type=F32)


def pack_codes(codes_ref, exponents_ref, o_ref, x_ref, e_ref, sems):
    copies = [
        pltpu.make_async_copy(codes_ref, x_ref, sems.at[0]),
        pltpu.make_async_copy(exponents_ref, e_ref, sems.at[1]),
    ]
    for copy in copies:
        copy.start()
    row = lax.broadcasted_iota(jnp.int32, (QT, QT), 0)
    col = lax.broadcasted_iota(jnp.int32, (QT, QT), 1)
    for copy in copies:
        copy.wait()
    power = jnp.exp2(jnp.broadcast_to(e_ref[...], (QT, QT)).astype(F32))
    scale = jnp.where(row == col, power, 0.0).astype(BF)
    x = dot(scale, x_ref[...]).astype(BF)
    o_ref[0:QT] = x[:, 0:128]
    o_ref[QT : 2 * QT] = x[:, 128:256]
    tail = x[:, 256:288]
    src = lax.broadcasted_iota(jnp.int32, (32, 128), 0)
    dst = lax.broadcasted_iota(jnp.int32, (32, 128), 1)
    total = jnp.zeros((40, 128), F32)
    for j in range(4):
        place = jnp.where(dst == src + 32 * j, 1.0, 0.0).astype(BF)
        total += dot(tail, place)[40 * j : 40 * j + 40]
    o_ref[2 * QT : 360] = total.astype(BF)


def order_quarters(one, two, after, o_ref):
    del after
    same = lax.axis_index("zh") == lax.axis_index("zl")
    o_ref[0] = jnp.where(same, two[...], one[...])
    o_ref[1] = jnp.where(same, one[...], two[...])


def merge_codes(a_ref, b_ref, c_ref, d_ref, after1, after2, *outs):
    del after1, after2
    pieces = (a_ref, b_ref, c_ref, d_ref)
    src = lax.broadcasted_iota(jnp.int32, (512, 128), 0)
    dst = lax.broadcasted_iota(jnp.int32, (512, 128), 1)
    for q, o_ref in enumerate(outs):
        for j, ref in enumerate(pieces):
            o_ref[:, 256 * j : 256 * j + 128] = ref[q, 0:QT]
            o_ref[:, 256 * j + 128 : 256 * j + 256] = ref[q, QT : 2 * QT]
        tails = jnp.concatenate([ref[q, 2 * QT : 360] for ref in pieces], axis=1)
        groups = []
        for j in range(4):
            place = (src // 128 == dst // 32) & (src % 128 == 32 * j + dst % 32)
            groups.append(dot(tails, jnp.where(place, 1.0, 0.0).astype(BF)))
        o_ref[:, 1024:1152] = jnp.concatenate(groups, axis=0).astype(BF)


def own_place():
    c, y, x = lax.axis_index("c"), lax.axis_index("y"), lax.axis_index("x")
    return c, jnp.where(c == 0, x, y), jnp.where(c == 0, y, x)


def arrange_rows(own, ref, w_ref, sem):
    c, first, second = own_place()
    for i in range(4):
        s = lax.rem(second + 4 - ARRIVES[i], 4)
        for j in range(4):
            f = lax.rem(first + 4 - GATHER[j], 4)
            y, x = jnp.where(c == 0, s, f), jnp.where(c == 0, f, s)
            row = lax.rem(y, 2) * UNITS + x * PIECE

            @pl.when((lax.div(y, 2) == c) == own)
            def _():
                for at, to, n in ((0, 256 * j, 256), (256, 1024 + 32 * j, 32)):
                    pltpu.make_async_copy(
                        ref.at[pl.ds(pl.multiple_of(row + at, 32), n)], w_ref.at[pl.ds(i * UNITS + to, n)], sem
                    ).start()

    pltpu.make_async_copy(w_ref.at[: 2 * UNITS], w_ref.at[: 2 * UNITS], sem).wait()


def arrange_own(ref, w_ref, sem):
    arrange_rows(True, ref, w_ref, sem)


def arrange_other(ref, half_ref, w_ref, sem):
    del half_ref
    arrange_rows(False, ref, w_ref, sem)


def stage_own(ref, after, w_ref, sem):
    del after
    copy = pltpu.make_async_copy(ref, w_ref.at[:, : 2 * UNITS], sem)
    copy.start()
    copy.wait()


def stage_other(ref, half_ref, w_ref, sem):
    del half_ref
    copy = pltpu.make_async_copy(ref, w_ref.at[:, 2 * UNITS :], sem)
    copy.start()
    copy.wait()


def scaled(x):
    most = jnp.full((8, x.shape[1]), jnp.max(jnp.abs(x)))
    power = 13.0 - jnp.ceil(jnp.log(jnp.maximum(most, 1e-30)) * 1.4426950408889634)
    return x * jnp.exp2(power)[:1], power


def project_early(m0, m1, w_ref, o_ref):
    for n in range(0, UNITS, 256):
        to = min(n + 256, UNITS)
        x = jnp.concatenate([m0[...], m1[...]], axis=1)
        o_ref[:, n:to] = dot(x, w_ref[: 2 * UNITS, n:to])


def project_in(m2, m3, w_ref, early_ref, o_ref, send_ref):
    for n in range(0, UNITS, 256):
        to = min(n + 256, UNITS)
        x = jnp.concatenate([m2[...], m3[...]], axis=1)
        o_ref[:, n:to] = early_ref[:, n:to] + dot(x, w_ref[2 * UNITS :, n:to])
    send_ref[0:QT], send_ref[QT:] = scaled(o_ref[...])


def project_out(a_ref, w_ref, o0, o1, o2, o3, t_ref, tail_ref):
    for g in range(4):
        for n in range(0, UNITS, 256):
            to = min(n + 256, UNITS)
            part = dot(a_ref[...], w_ref[:, g * UNITS + n : g * UNITS + to])
            t_ref[g, n:to] = part[:128].T
            tail_ref[32 * g : 32 * g + 32, n:to] = part[128:]
    t_ref[4] = tail_ref[...].T
    c, first, _ = own_place()
    for rel, o in zip(STEPS, (o0, o1, o2, o3)):
        f = lax.rem(first + rel, 4)
        for s in range(4):
            at = pl.ds(pl.multiple_of(jnp.where(c == 0, s * 4 + f, f * 4 + s) * CHIP_COLS, 8), CHIP_COLS)
            for p in range(2):
                both = jnp.concatenate([t_ref[2 * p, at], t_ref[2 * p + 1, at]], axis=0)
                o[s, 144 * p : 144 * p + 144] = both.astype(o.dtype)
            o[s, 288:360] = t_ref[4, at].astype(o.dtype)


def add_first(a0, b0, c0, d0, a1, b1, c1, d1, o0, o1, o2, o3):
    _, _, second = own_place()
    for rel, o in zip(STEPS, (o0, o1, o2, o3)):
        s = lax.rem(second + rel, 4)
        total = [
            a[s] + b[s].astype(F32) + c[s].astype(F32) + d[s].astype(F32) for a, b, c, d in ((a0, b0, c0, d0), (a1, b1, c1, d1))
        ]
        o[...] = jnp.concatenate(total, axis=0).astype(o.dtype)


def add_second(a, b, c, d, keep, to_zl, to_c, to_czl):
    total = a[...] + b[...].astype(F32) + c[...].astype(F32) + d[...].astype(F32)
    zl = lax.axis_index("zl")
    tiles = total.reshape(10, CHIP_COLS, 128)
    lane = lax.broadcasted_iota(jnp.int32, (CHIP_COLS, 128), 1)

    def share(crel, z):
        g = 2 * crel + z
        tail = jnp.where(lane < 32, pltpu.roll(tiles[4], (128 - 32 * g) % 128, 1), pltpu.roll(tiles[9], (160 - 32 * g) % 128, 1))
        return tiles[g], tiles[5 + g], tail

    shares = []
    for crel in range(2):
        lo, hi = (jnp.concatenate(share(crel, z), axis=0) for z in range(2))
        shares.append((jnp.where(zl == 0, lo, hi), jnp.where(zl == 0, hi, lo)))
    keep[...] = shares[0][0]
    for ref, value in ((to_zl, shares[0][1]), (to_c, shares[1][0]), (to_czl, shares[1][1])):
        ref[0:216], ref[216:] = scaled(value)


def finish(keep, from_c, from_czl, from_zl, out_ref, o_ref, sem):
    c = lax.axis_index("c")
    whole = [ref[0:216] * jnp.exp2(-ref[216:])[:1] for ref in (from_zl, from_c, from_czl)]
    own, other = keep[...] + whole[0], whole[1] + whole[2]
    cores = jnp.where(c == 0, own, other), jnp.where(c == 0, other, own)
    parts = []
    for q in range(2):
        for v in cores:
            parts += [v[72 * q : 72 * q + 72], v[144:, 32 * q : 32 * q + 32]]
    o_ref[...] = jnp.concatenate(parts, axis=1)
    copy = pltpu.make_async_copy(o_ref, out_ref, sem)
    copy.start()
    copy.wait()


def shape(dims, dtype):
    return jax.ShapeDtypeStruct(dims, dtype)


def in_hbm(x):
    return pltpu.with_memory_space_constraint(x, pltpu.HBM)


def shards(codes, exponents, w_in, w_out):
    zh, zl = lax.axis_index("zh"), lax.axis_index("zl")
    swap = [(0, 1), (1, 0)]
    z = ("zh", "zl")
    w_in_other = lax.ppermute(w_in, "c", swap)
    w_out_other = lax.ppermute(w_out, "c", swap)
    w_in, w_out = in_hbm(w_in), in_hbm(w_out)

    packed = call(
        pack_codes,
        shape((360, 128), BF),
        [ANY] * 2,
        [pltpu.VMEM((QT, PIECE), BF), pltpu.VMEM((1, QT), jnp.int32), pltpu.SemaphoreType.DMA((2,))],
        name="pack_codes",
    )(in_hbm(codes), in_hbm(exponents[None, :]))
    one = lax.ppermute(packed, z, [(0, 1), (1, 2), (2, 0), (3, 3)])
    two = lax.ppermute(packed, z, [(2, 1), (3, 2), (1, 3), (0, 0)])
    dma, half = [pltpu.SemaphoreType.DMA], 4608 * 1152 * 2
    rows = call(arrange_own, pltpu.VMEM((4 * UNITS, UNITS), BF), [ANY], dma, nbytes=half, name="arrange_own")(w_in)
    piece = call(order_quarters, shape((2, 360, 128), BF), [VMEM, VMEM, ANY], name="order_quarters")(one, two, rows)
    around = [lax.ppermute(piece, YX, first_axis(k)) for k in GATHER[1:]]
    rows = call(
        arrange_other, pltpu.VMEM((4 * UNITS, UNITS), BF), [ANY, VMEM], dma, nbytes=half, alias={1: 0}, name="arrange_other"
    )(w_in_other, rows)
    quarter = shape((QT, UNITS), BF)
    merged = call(merge_codes, [quarter] * 2, [VMEM] * 4 + [ANY] * 2, name="merge_codes")(piece, *around, rows, w_out_other)
    around = [[lax.ppermute(m, YX, second_axis(k)) for k in GATHER[1:]] for m in merged]

    preacts, sends = [], []
    for q in range(2):
        cost = dict(flops=QT * 4608 * 1152, nbytes=2304 * 1152 * 2)
        early = call(project_early, shape((QT, UNITS), F32), [VMEM] * 3, name="project_early", **cost)(
            merged[q], around[q][GATHER[1:].index(2)], rows
        )
        near = [v for k, v in zip(GATHER[1:], around[q]) if k != 2]
        outs = [shape((QT, UNITS), F32), shape((QT + 8, UNITS), F32)]
        preact, send = call(project_in, outs, [VMEM] * 4, name="project_in", **cost)(*near, rows, early)
        preacts.append(preact)
        sends.append(send.astype(jnp.float16))
    gots = [lax.ppermute(send, "zh", swap) for send in sends]
    columns = call(stage_own, pltpu.VMEM((UNITS, 4 * UNITS), BF), [ANY] * 2, dma, nbytes=half, name="stage_own")(w_out, merged[0])
    columns = call(
        stage_other, pltpu.VMEM((UNITS, 4 * UNITS), BF), [ANY, VMEM], dma, nbytes=half, alias={1: 0}, name="stage_other"
    )(w_out_other, columns)

    scattered = []
    for preact, got in zip(preacts, gots):
        other = got[:QT].astype(F32) * jnp.exp2(-got[QT : QT + 1].astype(F32))
        activ = jax.nn.gelu(preact + other, approximate=True).astype(BF)
        part = (4, 360, 128)
        mine, *away = call(
            project_out,
            [shape(part, F32)] + [shape(part, BF)] * 3,
            [VMEM] * 2,
            [pltpu.VMEM((5, UNITS, 128), F32), pltpu.VMEM((128, UNITS), F32)],
            flops=2 * QT * 4608 * 1152,
            nbytes=4608 * 1152 * 2,
            vmem=12,
            name="project_out",
        )(activ, columns)
        scattered += [mine] + [lax.ppermute(v, YX, first_axis(k)) for k, v in zip(STEPS[1:], away)]
    part = (720, 128)
    mine, *away = call(add_first, [shape(part, F32)] + [shape(part, BF)] * 3, [VMEM] * 8, name="add_first")(*scattered)
    around = [lax.ppermute(v, YX, second_axis(k)) for k, v in zip(STEPS[1:], away)]
    away = [shape((224, 128), F32)] * 3
    keep, *away = call(add_second, [shape((216, 128), F32)] + away, [VMEM] * 4, name="add_second")(mine, *around)
    to_zl, to_c, to_czl = (v.astype(jnp.float16) for v in away)
    from_c = lax.ppermute(to_c, "c", swap)
    from_czl = lax.ppermute(to_czl, ("c", "zl"), [(0, 3), (1, 2), (2, 1), (3, 0)])
    from_zl = lax.ppermute(to_zl, "zl", swap)
    got = [v.astype(F32) for v in (from_c, from_czl, from_zl)]
    whole = (CHIP_COLS, 4 * QT)
    scratch = [pltpu.VMEM(whole, F32), pltpu.SemaphoreType.DMA]
    return call(finish, pltpu.HBM(whole, F32), [VMEM] * 4, scratch, out_specs=ANY, name="finish")(keep, *got).T


def solution(mesh):
    split = Mesh(mesh.devices.reshape(2, 2, 2, 4, 4), ("zh", "c", "zl", "y", "x"))
    batch, hidden = ("zh", "c"), ("zl", "y", "x")
    placed = (P(batch, hidden), P(batch), P(batch, hidden), P(hidden, batch))
    return jax.shard_map(shards, mesh=split, in_specs=placed, out_specs=P(None, batch + hidden), check_vma=False)
```

```python
import jax
import jax.numpy as jnp
from jax import lax
from jax.experimental import pallas as pl
from jax.experimental.pallas import tpu as pltpu
from jax.sharding import Mesh, PartitionSpec as P

BF, F32 = jnp.bfloat16, jnp.float32
QT = 160
PIECE = 288
UNITS = 1152
CHIP_COLS = 72
VMEM = pl.BlockSpec(memory_space=pltpu.VMEM)
ANY = pl.BlockSpec(memory_space=pl.ANY)
YX = ("c", "y", "x")
STEPS = (0, 2, 1, 3)
GATHER = (0, 3, 1, 2)
ARRIVES = (0, 2, 3, 1)


def first_axis(step):
    pairs = []
    for y in range(4):
        for x in range(4):
            pairs.append((y * 4 + x, y * 4 + (x + step) % 4))
            pairs.append((16 + y * 4 + x, 16 + (y + step) % 4 * 4 + x))
    return pairs


def second_axis(step):
    pairs = []
    for y in range(4):
        for x in range(4):
            pairs.append((y * 4 + x, (y + step) % 4 * 4 + x))
            pairs.append((16 + y * 4 + x, 16 + y * 4 + (x + step) % 4))
    return pairs


def call(kernel, outs, ins, scratch=(), flops=0, nbytes=0, vmem=8, alias={}, out_specs=None, name=None):
    return pl.pallas_call(
        kernel,
        out_shape=outs,
        in_specs=ins,
        out_specs=out_specs or jax.tree.map(lambda _: VMEM, outs),
        input_output_aliases=alias,
        scratch_shapes=list(scratch),
        compiler_params=pltpu.CompilerParams(vmem_limit_bytes=vmem * 2**20),
        cost_estimate=pl.CostEstimate(flops=flops, bytes_accessed=nbytes, transcendentals=0),
        name=name,
    )


def dot(a, b):
    return jnp.dot(a, b, preferred_element_type=F32)


def pack_codes(codes_ref, exponents_ref, o_ref, x_ref, e_ref, sems):
    copies = [
        pltpu.make_async_copy(codes_ref, x_ref, sems.at[0]),
        pltpu.make_async_copy(exponents_ref, e_ref, sems.at[1]),
    ]
    for copy in copies:
        copy.start()
    row = lax.broadcasted_iota(jnp.int32, (QT, QT), 0)
    col = lax.broadcasted_iota(jnp.int32, (QT, QT), 1)
    for copy in copies:
        copy.wait()
    power = jnp.exp2(jnp.broadcast_to(e_ref[...], (QT, QT)).astype(F32))
    scale = jnp.where(row == col, power, 0.0).astype(BF)
    x = dot(scale, x_ref[...]).astype(BF)
    o_ref[0:QT] = x[:, 0:128]
    o_ref[QT : 2 * QT] = x[:, 128:256]
    tail = x[:, 256:288]
    src = lax.broadcasted_iota(jnp.int32, (32, 128), 0)
    dst = lax.broadcasted_iota(jnp.int32, (32, 128), 1)
    total = jnp.zeros((40, 128), F32)
    for j in range(4):
        place = jnp.where(dst == src + 32 * j, 1.0, 0.0).astype(BF)
        total += dot(tail, place)[40 * j : 40 * j + 40]
    o_ref[2 * QT : 360] = total.astype(BF)


def order_quarters(one, two, after, o_ref):
    del after
    swapped = lax.axis_index("zl") == 1
    o_ref[0] = jnp.where(swapped, one[...], two[...])
    o_ref[1] = jnp.where(swapped, two[...], one[...])


def merge_codes(a_ref, b_ref, c_ref, d_ref, after1, after2, *outs):
    del after1, after2
    pieces = (a_ref, b_ref, c_ref, d_ref)
    src = lax.broadcasted_iota(jnp.int32, (512, 128), 0)
    dst = lax.broadcasted_iota(jnp.int32, (512, 128), 1)
    for q, o_ref in enumerate(outs):
        for j, ref in enumerate(pieces):
            o_ref[:, 256 * j : 256 * j + 128] = ref[q, 0:QT]
            o_ref[:, 256 * j + 128 : 256 * j + 256] = ref[q, QT : 2 * QT]
        tails = jnp.concatenate([ref[q, 2 * QT : 360] for ref in pieces], axis=1)
        groups = []
        for j in range(4):
            place = (src // 128 == dst // 32) & (src % 128 == 32 * j + dst % 32)
            groups.append(dot(tails, jnp.where(place, 1.0, 0.0).astype(BF)))
        o_ref[:, 1024:1152] = jnp.concatenate(groups, axis=0).astype(BF)


def own_place():
    c, y, x = lax.axis_index("c"), lax.axis_index("y"), lax.axis_index("x")
    return c, jnp.where(c == 0, x, y), jnp.where(c == 0, y, x)


def arrange_rows(own, ref, w_ref, sem):
    c, first, second = own_place()
    for i in range(4):
        s = lax.rem(second + 4 - ARRIVES[i], 4)
        for j in range(4):
            f = lax.rem(first + 4 - GATHER[j], 4)
            y, x = jnp.where(c == 0, s, f), jnp.where(c == 0, f, s)
            row = lax.rem(y, 2) * UNITS + x * PIECE

            @pl.when((lax.div(y, 2) == c) == own)
            def _():
                for at, to, n in ((0, 256 * j, 256), (256, 1024 + 32 * j, 32)):
                    pltpu.make_async_copy(
                        ref.at[pl.ds(pl.multiple_of(row + at, 32), n)], w_ref.at[pl.ds(i * UNITS + to, n)], sem
                    ).start()

    pltpu.make_async_copy(w_ref.at[: 2 * UNITS], w_ref.at[: 2 * UNITS], sem).wait()


def arrange_own(ref, w_ref, sem):
    arrange_rows(True, ref, w_ref, sem)


def arrange_other(ref, half_ref, w_ref, sem):
    del half_ref
    arrange_rows(False, ref, w_ref, sem)


def stage_own(ref, after, w_ref, sem):
    del after
    copy = pltpu.make_async_copy(ref, w_ref.at[:, : 2 * UNITS], sem)
    copy.start()
    copy.wait()


def stage_other(ref, half_ref, w_ref, sem):
    del half_ref
    copy = pltpu.make_async_copy(ref, w_ref.at[:, 2 * UNITS :], sem)
    copy.start()
    copy.wait()


def scaled(x):
    most = jnp.full((8, x.shape[1]), jnp.max(jnp.abs(x)))
    power = 13.0 - jnp.ceil(jnp.log(jnp.maximum(most, 1e-30)) * 1.4426950408889634)
    return x * jnp.exp2(power)[:1], power


def project_early(m0, m1, w_ref, o_ref):
    for n in range(0, UNITS, 256):
        to = min(n + 256, UNITS)
        x = jnp.concatenate([m0[...], m1[...]], axis=1)
        o_ref[:, n:to] = dot(x, w_ref[: 2 * UNITS, n:to])


def project_in(m2, m3, w_ref, early_ref, o_ref, send_ref):
    for n in range(0, UNITS, 256):
        to = min(n + 256, UNITS)
        x = jnp.concatenate([m2[...], m3[...]], axis=1)
        o_ref[:, n:to] = early_ref[:, n:to] + dot(x, w_ref[2 * UNITS :, n:to])
    send_ref[0:QT], send_ref[QT:] = scaled(o_ref[...])


def project_out(a_ref, w_ref, o0, o1, o2, o3, t_ref, tail_ref):
    for g in range(4):
        for n in range(0, UNITS, 256):
            to = min(n + 256, UNITS)
            part = dot(a_ref[...], w_ref[:, g * UNITS + n : g * UNITS + to])
            t_ref[g, n:to] = part[:128].T
            tail_ref[32 * g : 32 * g + 32, n:to] = part[128:]
    t_ref[4] = tail_ref[...].T
    c, first, _ = own_place()
    for rel, o in zip(STEPS, (o0, o1, o2, o3)):
        f = lax.rem(first + rel, 4)
        for s in range(4):
            at = pl.ds(pl.multiple_of(jnp.where(c == 0, s * 4 + f, f * 4 + s) * CHIP_COLS, 8), CHIP_COLS)
            for p in range(2):
                both = jnp.concatenate([t_ref[2 * p, at], t_ref[2 * p + 1, at]], axis=0)
                o[s, 144 * p : 144 * p + 144] = both.astype(o.dtype)
            o[s, 288:360] = t_ref[4, at].astype(o.dtype)


def add_first(a0, b0, c0, d0, a1, b1, c1, d1, o0, o1, o2, o3):
    _, _, second = own_place()
    for rel, o in zip(STEPS, (o0, o1, o2, o3)):
        s = lax.rem(second + rel, 4)
        total = [
            a[s] + b[s].astype(F32) + c[s].astype(F32) + d[s].astype(F32) for a, b, c, d in ((a0, b0, c0, d0), (a1, b1, c1, d1))
        ]
        o[...] = jnp.concatenate(total, axis=0).astype(o.dtype)


def add_second(a, b, c, d, keep, to_zl, to_c, to_czl):
    total = a[...] + b[...].astype(F32) + c[...].astype(F32) + d[...].astype(F32)
    zl = lax.axis_index("zl")
    tiles = total.reshape(10, CHIP_COLS, 128)
    lane = lax.broadcasted_iota(jnp.int32, (CHIP_COLS, 128), 1)

    def share(crel, z):
        g = 2 * crel + z
        tail = jnp.where(lane < 32, pltpu.roll(tiles[4], (128 - 32 * g) % 128, 1), pltpu.roll(tiles[9], (160 - 32 * g) % 128, 1))
        return tiles[g], tiles[5 + g], tail

    shares = []
    for crel in range(2):
        lo, hi = (jnp.concatenate(share(crel, z), axis=0) for z in range(2))
        shares.append((jnp.where(zl == 0, lo, hi), jnp.where(zl == 0, hi, lo)))
    keep[...] = shares[0][0]
    for ref, value in ((to_zl, shares[0][1]), (to_c, shares[1][0]), (to_czl, shares[1][1])):
        ref[0:216], ref[216:] = scaled(value)


def finish(keep, from_c, from_czl, from_zl, out_ref, o_ref, sem):
    c = lax.axis_index("c")
    whole = [ref[0:216] * jnp.exp2(-ref[216:])[:1] for ref in (from_zl, from_c, from_czl)]
    own, other = keep[...] + whole[0], whole[1] + whole[2]
    cores = jnp.where(c == 0, own, other), jnp.where(c == 0, other, own)
    parts = []
    for q in range(2):
        for v in cores:
            parts += [v[72 * q : 72 * q + 72], v[144:, 32 * q : 32 * q + 32]]
    o_ref[...] = jnp.concatenate(parts, axis=1)
    copy = pltpu.make_async_copy(o_ref, out_ref, sem)
    copy.start()
    copy.wait()


def shape(dims, dtype):
    return jax.ShapeDtypeStruct(dims, dtype)


def in_hbm(x):
    return pltpu.with_memory_space_constraint(x, pltpu.HBM)


def shards(codes, exponents, w_in, w_out):
    zh, zl = lax.axis_index("zh"), lax.axis_index("zl")
    swap = [(0, 1), (1, 0)]
    z = ("zh", "zl")
    w_in_other = lax.ppermute(w_in, "c", swap)
    w_out_other = lax.ppermute(w_out, "c", swap)
    w_in, w_out = in_hbm(w_in), in_hbm(w_out)

    packed = call(
        pack_codes,
        shape((360, 128), BF),
        [ANY] * 2,
        [pltpu.VMEM((QT, PIECE), BF), pltpu.VMEM((1, QT), jnp.int32), pltpu.SemaphoreType.DMA((2,))],
        name="pack_codes",
    )(in_hbm(codes), in_hbm(exponents[None, :]))
    one = lax.ppermute(packed, z, [(0, 1), (3, 2), (2, 0), (1, 3)])
    two = lax.ppermute(packed, z, [(2, 1), (1, 2), (0, 0), (3, 3)])
    dma, half = [pltpu.SemaphoreType.DMA], 4608 * 1152 * 2
    rows = call(arrange_own, pltpu.VMEM((4 * UNITS, UNITS), BF), [ANY], dma, nbytes=half, name="arrange_own")(w_in)
    piece = call(order_quarters, shape((2, 360, 128), BF), [VMEM, VMEM, ANY], name="order_quarters")(one, two, rows)
    around = [lax.ppermute(piece, YX, first_axis(k)) for k in GATHER[1:]]
    rows = call(
        arrange_other, pltpu.VMEM((4 * UNITS, UNITS), BF), [ANY, VMEM], dma, nbytes=half, alias={1: 0}, name="arrange_other"
    )(w_in_other, rows)
    quarter = shape((QT, UNITS), BF)
    merged = call(merge_codes, [quarter] * 2, [VMEM] * 4 + [ANY] * 2, name="merge_codes")(piece, *around, rows, w_out_other)
    around = [[lax.ppermute(m, YX, second_axis(k)) for k in GATHER[1:]] for m in merged]

    preacts, sends = [], []
    for q in range(2):
        cost = dict(flops=QT * 4608 * 1152, nbytes=2304 * 1152 * 2)
        early = call(project_early, shape((QT, UNITS), F32), [VMEM] * 3, name="project_early", **cost)(
            merged[q], around[q][GATHER[1:].index(2)], rows
        )
        near = [v for k, v in zip(GATHER[1:], around[q]) if k != 2]
        outs = [shape((QT, UNITS), F32), shape((QT + 8, UNITS), F32)]
        preact, send = call(project_in, outs, [VMEM] * 4, name="project_in", **cost)(*near, rows, early)
        preacts.append(preact)
        sends.append(send.astype(jnp.float16))
    gots = [lax.ppermute(send, "zh", swap) for send in sends]
    columns = call(stage_own, pltpu.VMEM((UNITS, 4 * UNITS), BF), [ANY] * 2, dma, nbytes=half, name="stage_own")(w_out, merged[0])
    columns = call(
        stage_other, pltpu.VMEM((UNITS, 4 * UNITS), BF), [ANY, VMEM], dma, nbytes=half, alias={1: 0}, name="stage_other"
    )(w_out_other, columns)

    scattered = []
    for preact, got in zip(preacts, gots):
        other = got[:QT].astype(F32) * jnp.exp2(-got[QT : QT + 1].astype(F32))
        activ = jax.nn.gelu(preact + other, approximate=True).astype(BF)
        part = (4, 360, 128)
        mine, *away = call(
            project_out,
            [shape(part, F32)] + [shape(part, BF)] * 3,
            [VMEM] * 2,
            [pltpu.VMEM((5, UNITS, 128), F32), pltpu.VMEM((128, UNITS), F32)],
            flops=2 * QT * 4608 * 1152,
            nbytes=4608 * 1152 * 2,
            vmem=12,
            name="project_out",
        )(activ, columns)
        scattered += [mine] + [lax.ppermute(v, YX, first_axis(k)) for k, v in zip(STEPS[1:], away)]
    part = (720, 128)
    mine, *away = call(add_first, [shape(part, F32)] + [shape(part, BF)] * 3, [VMEM] * 8, name="add_first")(*scattered)
    around = [lax.ppermute(v, YX, second_axis(k)) for k, v in zip(STEPS[1:], away)]
    away = [shape((224, 128), F32)] * 3
    keep, *away = call(add_second, [shape((216, 128), F32)] + away, [VMEM] * 4, name="add_second")(mine, *around)
    to_zl, to_c, to_czl = (v.astype(jnp.float16) for v in away)
    from_c = lax.ppermute(to_c, "c", swap)
    from_czl = lax.ppermute(to_czl, ("c", "zl"), [(0, 3), (1, 2), (2, 1), (3, 0)])
    from_zl = lax.ppermute(to_zl, "zl", swap)
    got = [v.astype(F32) for v in (from_c, from_czl, from_zl)]
    whole = (CHIP_COLS, 4 * QT)
    scratch = [pltpu.VMEM(whole, F32), pltpu.SemaphoreType.DMA]
    return call(finish, pltpu.HBM(whole, F32), [VMEM] * 4, scratch, out_specs=ANY, name="finish")(keep, *got).T


def solution(mesh):
    split = Mesh(mesh.devices.reshape(2, 2, 2, 4, 4), ("zh", "c", "zl", "y", "x"))
    batch, hidden = ("zh", "c"), ("zl", "y", "x")
    placed = (P(batch, hidden), P(batch), P(batch, hidden), P(hidden, batch))
    return jax.shard_map(shards, mesh=split, in_specs=placed, out_specs=P(None, batch + hidden), check_vma=False)
```

```python
import jax
import jax.numpy as jnp
from jax import lax
from jax.experimental import pallas as pl
from jax.experimental.pallas import tpu as pltpu
from jax.sharding import Mesh, PartitionSpec as P

BF, F32 = jnp.bfloat16, jnp.float32
QT = 160
PIECE = 288
UNITS = 1152
CHIP_COLS = 72
VMEM = pl.BlockSpec(memory_space=pltpu.VMEM)
ANY = pl.BlockSpec(memory_space=pl.ANY)
YX = ("c", "y", "x")
STEPS = (0, 2, 1, 3)
GATHER = (0, 3, 1, 2)
ARRIVES = (0, 2, 3, 1)


def second_axis(step):
    pairs = []
    for y in range(4):
        for x in range(4):
            pairs.append((y * 4 + x, y * 4 + (x + step) % 4))
            pairs.append((16 + y * 4 + x, 16 + (y + step) % 4 * 4 + x))
    return pairs


def first_axis(step):
    pairs = []
    for y in range(4):
        for x in range(4):
            pairs.append((y * 4 + x, (y + step) % 4 * 4 + x))
            pairs.append((16 + y * 4 + x, 16 + y * 4 + (x + step) % 4))
    return pairs


def call(kernel, outs, ins, scratch=(), flops=0, nbytes=0, vmem=8, alias={}, out_specs=None, name=None):
    return pl.pallas_call(
        kernel,
        out_shape=outs,
        in_specs=ins,
        out_specs=out_specs or jax.tree.map(lambda _: VMEM, outs),
        input_output_aliases=alias,
        scratch_shapes=list(scratch),
        compiler_params=pltpu.CompilerParams(vmem_limit_bytes=vmem * 2**20),
        cost_estimate=pl.CostEstimate(flops=flops, bytes_accessed=nbytes, transcendentals=0),
        name=name,
    )


def dot(a, b):
    return jnp.dot(a, b, preferred_element_type=F32)


def pack_codes(codes_ref, exponents_ref, o_ref, x_ref, e_ref, sems):
    copies = [
        pltpu.make_async_copy(codes_ref, x_ref, sems.at[0]),
        pltpu.make_async_copy(exponents_ref, e_ref, sems.at[1]),
    ]
    for copy in copies:
        copy.start()
    row = lax.broadcasted_iota(jnp.int32, (QT, QT), 0)
    col = lax.broadcasted_iota(jnp.int32, (QT, QT), 1)
    for copy in copies:
        copy.wait()
    power = jnp.exp2(jnp.broadcast_to(e_ref[...], (QT, QT)).astype(F32))
    scale = jnp.where(row == col, power, 0.0).astype(BF)
    x = dot(scale, x_ref[...]).astype(BF)
    o_ref[0:QT] = x[:, 0:128]
    o_ref[QT : 2 * QT] = x[:, 128:256]
    tail = x[:, 256:288]
    src = lax.broadcasted_iota(jnp.int32, (32, 128), 0)
    dst = lax.broadcasted_iota(jnp.int32, (32, 128), 1)
    total = jnp.zeros((40, 128), F32)
    for j in range(4):
        place = jnp.where(dst == src + 32 * j, 1.0, 0.0).astype(BF)
        total += dot(tail, place)[40 * j : 40 * j + 40]
    o_ref[2 * QT : 360] = total.astype(BF)


def order_quarters(one, two, after, o_ref):
    del after
    swapped = lax.axis_index("zl") == 1
    o_ref[0] = jnp.where(swapped, one[...], two[...])
    o_ref[1] = jnp.where(swapped, two[...], one[...])


def merge_codes(a_ref, b_ref, c_ref, d_ref, after1, after2, *outs):
    del after1, after2
    pieces = (a_ref, b_ref, c_ref, d_ref)
    for q, o_ref in enumerate(outs):
        for j, ref in enumerate(pieces):
            o_ref[:, 256 * j : 256 * j + 128] = ref[q, 0:QT]
            o_ref[:, 256 * j + 128 : 256 * j + 256] = ref[q, QT : 2 * QT]
        tails = [ref[q, 2 * QT : 360].astype(F32) for ref in pieces]
        groups = [jnp.concatenate([t[:, 32 * j : 32 * j + 32] for t in tails], axis=1) for j in range(4)]
        o_ref[:, 1024:1152] = jnp.concatenate(groups, axis=0).astype(BF)


def own_place():
    c, y, x = lax.axis_index("c"), lax.axis_index("y"), lax.axis_index("x")
    return c, jnp.where(c == 0, y, x), jnp.where(c == 0, x, y)


def arrange_rows(own, ref, w_ref, sem):
    c, first, second = own_place()
    for i in range(4):
        s = lax.rem(second + 4 - ARRIVES[i], 4)
        for j in range(4):
            f = lax.rem(first + 4 - GATHER[j], 4)
            y, x = jnp.where(c == 0, f, s), jnp.where(c == 0, s, f)
            row = lax.rem(y, 2) * UNITS + x * PIECE

            @pl.when((lax.div(y, 2) == c) == own)
            def _():
                for at, to, n in ((0, 256 * j, 256), (256, 1024 + 32 * j, 32)):
                    pltpu.make_async_copy(
                        ref.at[pl.ds(pl.multiple_of(row + at, 32), n)], w_ref.at[pl.ds(i * UNITS + to, n)], sem
                    ).start()

    pltpu.make_async_copy(w_ref.at[: 2 * UNITS], w_ref.at[: 2 * UNITS], sem).wait()


def arrange_own(ref, w_ref, sem):
    arrange_rows(True, ref, w_ref, sem)


def arrange_other(ref, half_ref, w_ref, sem):
    del half_ref
    arrange_rows(False, ref, w_ref, sem)


def stage_own(ref, after, w_ref, sem):
    del after
    copy = pltpu.make_async_copy(ref, w_ref.at[:, : 2 * UNITS], sem)
    copy.start()
    copy.wait()


def stage_other(ref, half_ref, w_ref, sem):
    del half_ref
    copy = pltpu.make_async_copy(ref, w_ref.at[:, 2 * UNITS :], sem)
    copy.start()
    copy.wait()


def scaled(x):
    most = jnp.full((8, x.shape[1]), jnp.max(jnp.abs(x)))
    power = 13.0 - jnp.ceil(jnp.log(jnp.maximum(most, 1e-30)) * 1.4426950408889634)
    return x * jnp.exp2(power)[:1], power


def project_early(m0, m1, w_ref, o_ref):
    for n in range(0, UNITS, 256):
        to = min(n + 256, UNITS)
        x = jnp.concatenate([m0[...], m1[...]], axis=1)
        o_ref[:, n:to] = dot(x, w_ref[: 2 * UNITS, n:to])


def project_in(m2, m3, w_ref, early_ref, o_ref, send_ref):
    for n in range(0, UNITS, 256):
        to = min(n + 256, UNITS)
        x = jnp.concatenate([m2[...], m3[...]], axis=1)
        o_ref[:, n:to] = early_ref[:, n:to] + dot(x, w_ref[2 * UNITS :, n:to])
    send_ref[0:QT], send_ref[QT:] = scaled(o_ref[...])


def project_out(a_ref, w_ref, o0, o1, o2, o3, t_ref, tail_ref):
    for g in range(4):
        for n in range(0, UNITS, 256):
            to = min(n + 256, UNITS)
            part = dot(a_ref[...], w_ref[:, g * UNITS + n : g * UNITS + to])
            t_ref[g, n:to] = part[:128].T
            tail_ref[32 * g : 32 * g + 32, n:to] = part[128:]
    t_ref[4] = tail_ref[...].T
    c, first, _ = own_place()
    for rel, o in zip(STEPS, (o0, o1, o2, o3)):
        f = lax.rem(first + rel, 4)
        for s in range(4):
            at = pl.ds(pl.multiple_of(jnp.where(c == 0, f * 4 + s, s * 4 + f) * CHIP_COLS, 8), CHIP_COLS)
            for p in range(2):
                both = jnp.concatenate([t_ref[2 * p, at], t_ref[2 * p + 1, at]], axis=0)
                o[s, 144 * p : 144 * p + 144] = both.astype(o.dtype)
            o[s, 288:360] = t_ref[4, at].astype(o.dtype)


def add_first(a0, b0, c0, d0, a1, b1, c1, d1, o0, o1, o2, o3):
    _, _, second = own_place()
    for rel, o in zip(STEPS, (o0, o1, o2, o3)):
        s = lax.rem(second + rel, 4)
        total = [
            a[s] + b[s].astype(F32) + c[s].astype(F32) + d[s].astype(F32) for a, b, c, d in ((a0, b0, c0, d0), (a1, b1, c1, d1))
        ]
        o[...] = jnp.concatenate(total, axis=0).astype(o.dtype)


def add_second(a, b, c, d, keep, to_zl, to_c, to_czl):
    total = a[...] + b[...].astype(F32) + c[...].astype(F32) + d[...].astype(F32)
    zl = lax.axis_index("zl")
    tiles = total.reshape(10, CHIP_COLS, 128)
    lane = lax.broadcasted_iota(jnp.int32, (CHIP_COLS, 128), 1)

    def share(crel, z):
        g = 2 * crel + z
        tail = jnp.where(lane < 32, pltpu.roll(tiles[4], (128 - 32 * g) % 128, 1), pltpu.roll(tiles[9], (160 - 32 * g) % 128, 1))
        return tiles[g], tiles[5 + g], tail

    shares = []
    for crel in range(2):
        lo, hi = (jnp.concatenate(share(crel, z), axis=0) for z in range(2))
        shares.append((jnp.where(zl == 0, lo, hi), jnp.where(zl == 0, hi, lo)))
    keep[...] = shares[0][0]
    for ref, value in ((to_zl, shares[0][1]), (to_c, shares[1][0]), (to_czl, shares[1][1])):
        ref[0:216], ref[216:] = scaled(value)


def finish(keep, from_c, from_czl, from_zl, out_ref, o_ref, sem):
    c = lax.axis_index("c")
    whole = [ref[0:216] * jnp.exp2(-ref[216:])[:1] for ref in (from_zl, from_c, from_czl)]
    own, other = keep[...] + whole[0], whole[1] + whole[2]
    cores = jnp.where(c == 0, own, other), jnp.where(c == 0, other, own)
    parts = []
    for q in range(2):
        for v in cores:
            parts += [v[72 * q : 72 * q + 72], v[144:, 32 * q : 32 * q + 32]]
    o_ref[...] = jnp.concatenate(parts, axis=1)
    copy = pltpu.make_async_copy(o_ref, out_ref, sem)
    copy.start()
    copy.wait()


def shape(dims, dtype):
    return jax.ShapeDtypeStruct(dims, dtype)


def in_hbm(x):
    return pltpu.with_memory_space_constraint(x, pltpu.HBM)


def shards(codes, exponents, w_in, w_out):
    zh, zl = lax.axis_index("zh"), lax.axis_index("zl")
    swap = [(0, 1), (1, 0)]
    z = ("zh", "zl")
    w_in_other = lax.ppermute(w_in, "c", swap)
    w_out_other = lax.ppermute(w_out, "c", swap)
    w_in, w_out = in_hbm(w_in), in_hbm(w_out)

    packed = call(
        pack_codes,
        shape((360, 128), BF),
        [ANY] * 2,
        [pltpu.VMEM((QT, PIECE), BF), pltpu.VMEM((1, QT), jnp.int32), pltpu.SemaphoreType.DMA((2,))],
        name="pack_codes",
    )(in_hbm(codes), in_hbm(exponents[None, :]))
    one = lax.ppermute(packed, z, [(0, 1), (3, 2), (2, 0), (1, 3)])
    two = lax.ppermute(packed, z, [(2, 1), (1, 2), (0, 0), (3, 3)])
    dma, half = [pltpu.SemaphoreType.DMA], 4608 * 1152 * 2
    rows = call(arrange_own, pltpu.VMEM((4 * UNITS, UNITS), BF), [ANY], dma, nbytes=half, name="arrange_own")(w_in)
    piece = call(order_quarters, shape((2, 360, 128), BF), [VMEM, VMEM, ANY], name="order_quarters")(one, two, rows)
    around = [lax.ppermute(piece, YX, first_axis(k)) for k in GATHER[1:]]
    rows = call(
        arrange_other, pltpu.VMEM((4 * UNITS, UNITS), BF), [ANY, VMEM], dma, nbytes=half, alias={1: 0}, name="arrange_other"
    )(w_in_other, rows)
    quarter = shape((QT, UNITS), BF)
    merged = call(merge_codes, [quarter] * 2, [VMEM] * 4 + [ANY] * 2, name="merge_codes")(piece, *around, rows, w_out_other)
    around = [[lax.ppermute(m, YX, second_axis(k)) for k in GATHER[1:]] for m in merged]

    preacts, sends = [], []
    for q in range(2):
        cost = dict(flops=QT * 4608 * 1152, nbytes=2304 * 1152 * 2)
        early = call(project_early, shape((QT, UNITS), F32), [VMEM] * 3, name="project_early", **cost)(
            merged[q], around[q][GATHER[1:].index(2)], rows
        )
        near = [v for k, v in zip(GATHER[1:], around[q]) if k != 2]
        outs = [shape((QT, UNITS), F32), shape((QT + 8, UNITS), F32)]
        preact, send = call(project_in, outs, [VMEM] * 4, name="project_in", **cost)(*near, rows, early)
        preacts.append(preact)
        sends.append(send.astype(jnp.float16))
    gots = [lax.ppermute(send, "zh", swap) for send in sends]
    columns = call(stage_own, pltpu.VMEM((UNITS, 4 * UNITS), BF), [ANY] * 2, dma, nbytes=half, name="stage_own")(w_out, rows)
    columns = call(
        stage_other, pltpu.VMEM((UNITS, 4 * UNITS), BF), [ANY, VMEM], dma, nbytes=half, alias={1: 0}, name="stage_other"
    )(w_out_other, columns)

    scattered = []
    for preact, got in zip(preacts, gots):
        other = got[:QT].astype(F32) * jnp.exp2(-got[QT : QT + 1].astype(F32))
        activ = jax.nn.gelu(preact + other, approximate=True).astype(BF)
        part = (4, 360, 128)
        mine, *away = call(
            project_out,
            [shape(part, F32)] + [shape(part, BF)] * 3,
            [VMEM] * 2,
            [pltpu.VMEM((5, UNITS, 128), F32), pltpu.VMEM((128, UNITS), F32)],
            flops=2 * QT * 4608 * 1152,
            nbytes=4608 * 1152 * 2,
            vmem=12,
            name="project_out",
        )(activ, columns)
        scattered += [mine] + [lax.ppermute(v, YX, first_axis(k)) for k, v in zip(STEPS[1:], away)]
    part = (720, 128)
    mine, *away = call(add_first, [shape(part, F32)] + [shape(part, BF)] * 3, [VMEM] * 8, name="add_first")(*scattered)
    around = [lax.ppermute(v, YX, second_axis(k)) for k, v in zip(STEPS[1:], away)]
    away = [shape((224, 128), F32)] * 3
    keep, *away = call(add_second, [shape((216, 128), F32)] + away, [VMEM] * 4, name="add_second")(mine, *around)
    to_zl, to_c, to_czl = (v.astype(jnp.float16) for v in away)
    from_c = lax.ppermute(to_c, "c", swap)
    from_czl = lax.ppermute(to_czl, ("c", "zl"), [(0, 3), (1, 2), (2, 1), (3, 0)])
    from_zl = lax.ppermute(to_zl, "zl", swap)
    got = [v.astype(F32) for v in (from_c, from_czl, from_zl)]
    whole = (CHIP_COLS, 4 * QT)
    scratch = [pltpu.VMEM(whole, F32), pltpu.SemaphoreType.DMA]
    return call(finish, pltpu.HBM(whole, F32), [VMEM] * 4, scratch, out_specs=ANY, name="finish")(keep, *got).T


def solution(mesh):
    split = Mesh(mesh.devices.reshape(2, 2, 2, 4, 4), ("zh", "c", "zl", "y", "x"))
    batch, hidden = ("zh", "c"), ("zl", "y", "x")
    placed = (P(batch, hidden), P(batch), P(batch, hidden), P(hidden, batch))
    return jax.shard_map(shards, mesh=split, in_specs=placed, out_specs=P(None, batch + hidden), check_vma=False)
```

```python
import jax
import jax.numpy as jnp
from jax import lax
from jax.experimental import pallas as pl
from jax.experimental.pallas import tpu as pltpu
from jax.sharding import Mesh, PartitionSpec as P

BF, F32 = jnp.bfloat16, jnp.float32
QT = 160
PIECE = 288
UNITS = 1152
CHIP_COLS = 72
VMEM = pl.BlockSpec(memory_space=pltpu.VMEM)
ANY = pl.BlockSpec(memory_space=pl.ANY)
YX = ("c", "y", "x")
STEPS = (0, 2, 1, 3)
GATHER = (0, 3, 1, 2)
ARRIVES = (0, 2, 3, 1)


def second_axis(step):
    pairs = []
    for y in range(4):
        for x in range(4):
            pairs.append((y * 4 + x, y * 4 + (x + step) % 4))
            pairs.append((16 + y * 4 + x, 16 + (y + step) % 4 * 4 + x))
    return pairs


def first_axis(step):
    pairs = []
    for y in range(4):
        for x in range(4):
            pairs.append((y * 4 + x, (y + step) % 4 * 4 + x))
            pairs.append((16 + y * 4 + x, 16 + y * 4 + (x + step) % 4))
    return pairs


def call(kernel, outs, ins, scratch=(), flops=0, nbytes=0, vmem=8, alias={}, out_specs=None, name=None):
    return pl.pallas_call(
        kernel,
        out_shape=outs,
        in_specs=ins,
        out_specs=out_specs or jax.tree.map(lambda _: VMEM, outs),
        input_output_aliases=alias,
        scratch_shapes=list(scratch),
        compiler_params=pltpu.CompilerParams(vmem_limit_bytes=vmem * 2**20),
        cost_estimate=pl.CostEstimate(flops=flops, bytes_accessed=nbytes, transcendentals=0),
        name=name,
    )


def dot(a, b):
    return jnp.dot(a, b, preferred_element_type=F32)


def pack_codes(codes_ref, exponents_ref, o_ref, x_ref, e_ref, sems):
    copies = [
        pltpu.make_async_copy(codes_ref, x_ref, sems.at[0]),
        pltpu.make_async_copy(exponents_ref, e_ref, sems.at[1]),
    ]
    for copy in copies:
        copy.start()
    row = lax.broadcasted_iota(jnp.int32, (QT, QT), 0)
    col = lax.broadcasted_iota(jnp.int32, (QT, QT), 1)
    for copy in copies:
        copy.wait()
    power = jnp.exp2(jnp.broadcast_to(e_ref[...], (QT, QT)).astype(F32))
    scale = jnp.where(row == col, power, 0.0).astype(BF)
    x = dot(scale, x_ref[...]).astype(BF)
    o_ref[0:QT] = x[:, 0:128]
    o_ref[QT : 2 * QT] = x[:, 128:256]
    tail = x[:, 256:288].astype(F32)
    o_ref[2 * QT : 360] = jnp.concatenate([tail[40 * j : 40 * j + 40] for j in range(4)], axis=1).astype(BF)


def order_quarters(one, two, after, o_ref):
    del after
    swapped = lax.axis_index("zl") == 1
    o_ref[0] = jnp.where(swapped, one[...], two[...])
    o_ref[1] = jnp.where(swapped, two[...], one[...])


def merge_codes(a_ref, b_ref, c_ref, d_ref, after1, after2, *outs):
    del after1, after2
    pieces = (a_ref, b_ref, c_ref, d_ref)
    for q, o_ref in enumerate(outs):
        for j, ref in enumerate(pieces):
            o_ref[:, 256 * j : 256 * j + 128] = ref[q, 0:QT]
            o_ref[:, 256 * j + 128 : 256 * j + 256] = ref[q, QT : 2 * QT]
        tails = [ref[q, 2 * QT : 360].astype(F32) for ref in pieces]
        groups = [jnp.concatenate([t[:, 32 * j : 32 * j + 32] for t in tails], axis=1) for j in range(4)]
        o_ref[:, 1024:1152] = jnp.concatenate(groups, axis=0).astype(BF)


def own_place():
    c, y, x = lax.axis_index("c"), lax.axis_index("y"), lax.axis_index("x")
    return c, jnp.where(c == 0, y, x), jnp.where(c == 0, x, y)


def arrange_rows(own, ref, w_ref, sem):
    c, first, second = own_place()
    for i in range(4):
        s = lax.rem(second + 4 - ARRIVES[i], 4)
        for j in range(4):
            f = lax.rem(first + 4 - GATHER[j], 4)
            y, x = jnp.where(c == 0, f, s), jnp.where(c == 0, s, f)
            row = lax.rem(y, 2) * UNITS + x * PIECE

            @pl.when((lax.div(y, 2) == c) == own)
            def _():
                for at, to, n in ((0, 256 * j, 256), (256, 1024 + 32 * j, 32)):
                    pltpu.make_async_copy(
                        ref.at[pl.ds(pl.multiple_of(row + at, 32), n)], w_ref.at[pl.ds(i * UNITS + to, n)], sem
                    ).start()

    pltpu.make_async_copy(w_ref.at[: 2 * UNITS], w_ref.at[: 2 * UNITS], sem).wait()


def arrange_own(ref, w_ref, sem):
    arrange_rows(True, ref, w_ref, sem)


def arrange_other(ref, half_ref, w_ref, sem):
    del half_ref
    arrange_rows(False, ref, w_ref, sem)


def stage_own(ref, after, w_ref, sem):
    del after
    copy = pltpu.make_async_copy(ref, w_ref.at[:, : 2 * UNITS], sem)
    copy.start()
    copy.wait()


def stage_other(ref, half_ref, w_ref, sem):
    del half_ref
    copy = pltpu.make_async_copy(ref, w_ref.at[:, 2 * UNITS :], sem)
    copy.start()
    copy.wait()


def scaled(x):
    most = jnp.full((8, x.shape[1]), jnp.max(jnp.abs(x)))
    power = 13.0 - jnp.ceil(jnp.log(jnp.maximum(most, 1e-30)) * 1.4426950408889634)
    return x * jnp.exp2(power)[:1], power


def project_early(m0, m1, w_ref, o_ref):
    for n in range(0, UNITS, 256):
        to = min(n + 256, UNITS)
        x = jnp.concatenate([m0[...], m1[...]], axis=1)
        o_ref[:, n:to] = dot(x, w_ref[: 2 * UNITS, n:to])


def project_in(m2, m3, w_ref, early_ref, o_ref, send_ref):
    for n in range(0, UNITS, 256):
        to = min(n + 256, UNITS)
        x = jnp.concatenate([m2[...], m3[...]], axis=1)
        o_ref[:, n:to] = early_ref[:, n:to] + dot(x, w_ref[2 * UNITS :, n:to])
    send_ref[0:QT], send_ref[QT:] = scaled(o_ref[...])


def project_out(a_ref, w_ref, o0, o1, o2, o3, t_ref, tail_ref):
    for g in range(4):
        for n in range(0, UNITS, 256):
            to = min(n + 256, UNITS)
            part = dot(a_ref[...], w_ref[:, g * UNITS + n : g * UNITS + to])
            t_ref[g, n:to] = part[:128].T
            tail_ref[32 * g : 32 * g + 32, n:to] = part[128:]
    t_ref[4] = tail_ref[...].T
    c, first, _ = own_place()
    for rel, o in zip(STEPS, (o0, o1, o2, o3)):
        f = lax.rem(first + rel, 4)
        for s in range(4):
            at = pl.ds(pl.multiple_of(jnp.where(c == 0, f * 4 + s, s * 4 + f) * CHIP_COLS, 8), CHIP_COLS)
            for p in range(2):
                both = jnp.concatenate([t_ref[2 * p, at], t_ref[2 * p + 1, at]], axis=0)
                o[s, 144 * p : 144 * p + 144] = both.astype(o.dtype)
            o[s, 288:360] = t_ref[4, at].astype(o.dtype)


def add_first(a0, b0, c0, d0, a1, b1, c1, d1, o0, o1, o2, o3):
    _, _, second = own_place()
    for rel, o in zip(STEPS, (o0, o1, o2, o3)):
        s = lax.rem(second + rel, 4)
        total = [
            a[s] + b[s].astype(F32) + c[s].astype(F32) + d[s].astype(F32) for a, b, c, d in ((a0, b0, c0, d0), (a1, b1, c1, d1))
        ]
        o[...] = jnp.concatenate(total, axis=0).astype(o.dtype)


def add_second(a, b, c, d, keep, to_zl, to_c, to_czl):
    total = a[...] + b[...].astype(F32) + c[...].astype(F32) + d[...].astype(F32)
    zl = lax.axis_index("zl")
    tiles = total.reshape(10, CHIP_COLS, 128)
    lane = lax.broadcasted_iota(jnp.int32, (CHIP_COLS, 128), 1)

    def share(crel, z):
        g = 2 * crel + z
        tail = jnp.where(lane < 32, pltpu.roll(tiles[4], (128 - 32 * g) % 128, 1), pltpu.roll(tiles[9], (160 - 32 * g) % 128, 1))
        return tiles[g], tiles[5 + g], tail

    shares = []
    for crel in range(2):
        lo, hi = (jnp.concatenate(share(crel, z), axis=0) for z in range(2))
        shares.append((jnp.where(zl == 0, lo, hi), jnp.where(zl == 0, hi, lo)))
    keep[...] = shares[0][0]
    for ref, value in ((to_zl, shares[0][1]), (to_c, shares[1][0]), (to_czl, shares[1][1])):
        ref[0:216], ref[216:] = scaled(value)


def finish(keep, from_c, from_czl, from_zl, out_ref, o_ref, sem):
    c = lax.axis_index("c")
    whole = [ref[0:216] * jnp.exp2(-ref[216:])[:1] for ref in (from_zl, from_c, from_czl)]
    own, other = keep[...] + whole[0], whole[1] + whole[2]
    cores = jnp.where(c == 0, own, other), jnp.where(c == 0, other, own)
    parts = []
    for q in range(2):
        for v in cores:
            parts += [v[72 * q : 72 * q + 72], v[144:, 32 * q : 32 * q + 32]]
    o_ref[...] = jnp.concatenate(parts, axis=1)
    copy = pltpu.make_async_copy(o_ref, out_ref, sem)
    copy.start()
    copy.wait()


def shape(dims, dtype):
    return jax.ShapeDtypeStruct(dims, dtype)


def in_hbm(x):
    return pltpu.with_memory_space_constraint(x, pltpu.HBM)


def shards(codes, exponents, w_in, w_out):
    zh, zl = lax.axis_index("zh"), lax.axis_index("zl")
    swap = [(0, 1), (1, 0)]
    z = ("zh", "zl")
    w_in_other = lax.ppermute(w_in, "c", swap)
    w_out_other = lax.ppermute(w_out, "c", swap)
    w_in, w_out = in_hbm(w_in), in_hbm(w_out)

    packed = call(
        pack_codes,
        shape((360, 128), BF),
        [ANY] * 2,
        [pltpu.VMEM((QT, PIECE), BF), pltpu.VMEM((1, QT), jnp.int32), pltpu.SemaphoreType.DMA((2,))],
        name="pack_codes",
    )(in_hbm(codes), in_hbm(exponents[None, :]))
    one = lax.ppermute(packed, z, [(0, 1), (3, 2), (2, 0), (1, 3)])
    two = lax.ppermute(packed, z, [(2, 1), (1, 2), (0, 0), (3, 3)])
    dma, half = [pltpu.SemaphoreType.DMA], 4608 * 1152 * 2
    rows = call(arrange_own, pltpu.VMEM((4 * UNITS, UNITS), BF), [ANY], dma, nbytes=half, name="arrange_own")(w_in)
    piece = call(order_quarters, shape((2, 360, 128), BF), [VMEM, VMEM, ANY], name="order_quarters")(one, two, rows)
    around = [lax.ppermute(piece, YX, first_axis(k)) for k in GATHER[1:]]
    rows = call(
        arrange_other, pltpu.VMEM((4 * UNITS, UNITS), BF), [ANY, VMEM], dma, nbytes=half, alias={1: 0}, name="arrange_other"
    )(w_in_other, rows)
    quarter = shape((QT, UNITS), BF)
    merged = call(merge_codes, [quarter] * 2, [VMEM] * 4 + [ANY] * 2, name="merge_codes")(piece, *around, rows, w_out_other)
    around = [[lax.ppermute(m, YX, second_axis(k)) for k in GATHER[1:]] for m in merged]

    preacts, sends = [], []
    for q in range(2):
        cost = dict(flops=QT * 4608 * 1152, nbytes=2304 * 1152 * 2)
        early = call(project_early, shape((QT, UNITS), F32), [VMEM] * 3, name="project_early", **cost)(
            merged[q], around[q][GATHER[1:].index(2)], rows
        )
        near = [v for k, v in zip(GATHER[1:], around[q]) if k != 2]
        outs = [shape((QT, UNITS), F32), shape((QT + 8, UNITS), F32)]
        preact, send = call(project_in, outs, [VMEM] * 4, name="project_in", **cost)(*near, rows, early)
        preacts.append(preact)
        sends.append(send.astype(jnp.float16))
    gots = [lax.ppermute(send, "zh", swap) for send in sends]
    columns = call(stage_own, pltpu.VMEM((UNITS, 4 * UNITS), BF), [ANY] * 2, dma, nbytes=half, name="stage_own")(w_out, rows)
    columns = call(
        stage_other, pltpu.VMEM((UNITS, 4 * UNITS), BF), [ANY, VMEM], dma, nbytes=half, alias={1: 0}, name="stage_other"
    )(w_out_other, columns)

    scattered = []
    for preact, got in zip(preacts, gots):
        other = got[:QT].astype(F32) * jnp.exp2(-got[QT : QT + 1].astype(F32))
        activ = jax.nn.gelu(preact + other, approximate=True).astype(BF)
        part = (4, 360, 128)
        mine, *away = call(
            project_out,
            [shape(part, F32)] + [shape(part, BF)] * 3,
            [VMEM] * 2,
            [pltpu.VMEM((5, UNITS, 128), F32), pltpu.VMEM((128, UNITS), F32)],
            flops=2 * QT * 4608 * 1152,
            nbytes=4608 * 1152 * 2,
            vmem=12,
            name="project_out",
        )(activ, columns)
        scattered += [mine] + [lax.ppermute(v, YX, first_axis(k)) for k, v in zip(STEPS[1:], away)]
    part = (720, 128)
    mine, *away = call(add_first, [shape(part, F32)] + [shape(part, BF)] * 3, [VMEM] * 8, name="add_first")(*scattered)
    around = [lax.ppermute(v, YX, second_axis(k)) for k, v in zip(STEPS[1:], away)]
    away = [shape((224, 128), F32)] * 3
    keep, *away = call(add_second, [shape((216, 128), F32)] + away, [VMEM] * 4, name="add_second")(mine, *around)
    to_zl, to_c, to_czl = (v.astype(jnp.float16) for v in away)
    from_c = lax.ppermute(to_c, "c", swap)
    from_czl = lax.ppermute(to_czl, ("c", "zl"), [(0, 3), (1, 2), (2, 1), (3, 0)])
    from_zl = lax.ppermute(to_zl, "zl", swap)
    got = [v.astype(F32) for v in (from_c, from_czl, from_zl)]
    whole = (CHIP_COLS, 4 * QT)
    scratch = [pltpu.VMEM(whole, F32), pltpu.SemaphoreType.DMA]
    return call(finish, pltpu.HBM(whole, F32), [VMEM] * 4, scratch, out_specs=ANY, name="finish")(keep, *got).T


def solution(mesh):
    split = Mesh(mesh.devices.reshape(2, 2, 2, 4, 4), ("zh", "c", "zl", "y", "x"))
    batch, hidden = ("zh", "c"), ("zl", "y", "x")
    placed = (P(batch, hidden), P(batch), P(batch, hidden), P(hidden, batch))
    return jax.shard_map(shards, mesh=split, in_specs=placed, out_specs=P(None, batch + hidden), check_vma=False)
```

```python
import jax
import jax.numpy as jnp
from jax import lax
from jax.experimental import pallas as pl
from jax.experimental.pallas import tpu as pltpu
from jax.sharding import Mesh, PartitionSpec as P

BF, F32 = jnp.bfloat16, jnp.float32
QT = 160
PIECE = 288
UNITS = 1152
CHIP_COLS = 72
VMEM = pl.BlockSpec(memory_space=pltpu.VMEM)
ANY = pl.BlockSpec(memory_space=pl.ANY)
YX = ("c", "y", "x")
STEPS = (0, 2, 1, 3)
GATHER = (0, 3, 1, 2)
ARRIVES = (0, 2, 3, 1)


def second_axis(step):
    pairs = []
    for y in range(4):
        for x in range(4):
            pairs.append((y * 4 + x, y * 4 + (x + step) % 4))
            pairs.append((16 + y * 4 + x, 16 + (y + step) % 4 * 4 + x))
    return pairs


def first_axis(step):
    pairs = []
    for y in range(4):
        for x in range(4):
            pairs.append((y * 4 + x, (y + step) % 4 * 4 + x))
            pairs.append((16 + y * 4 + x, 16 + y * 4 + (x + step) % 4))
    return pairs


def call(kernel, outs, ins, scratch=(), flops=0, nbytes=0, vmem=8, alias={}, out_specs=None, name=None):
    return pl.pallas_call(
        kernel,
        out_shape=outs,
        in_specs=ins,
        out_specs=out_specs or jax.tree.map(lambda _: VMEM, outs),
        input_output_aliases=alias,
        scratch_shapes=list(scratch),
        compiler_params=pltpu.CompilerParams(vmem_limit_bytes=vmem * 2**20),
        cost_estimate=pl.CostEstimate(flops=flops, bytes_accessed=nbytes, transcendentals=0),
        name=name,
    )


def dot(a, b):
    return jnp.dot(a, b, preferred_element_type=F32)


def pack_codes(codes_ref, exponents_ref, o_ref, x_ref, e_ref, sems):
    copies = [
        pltpu.make_async_copy(codes_ref, x_ref, sems.at[0]),
        pltpu.make_async_copy(exponents_ref, e_ref, sems.at[1]),
    ]
    for copy in copies:
        copy.start()
    row = lax.broadcasted_iota(jnp.int32, (QT, QT), 0)
    col = lax.broadcasted_iota(jnp.int32, (QT, QT), 1)
    for copy in copies:
        copy.wait()
    power = jnp.exp2(jnp.broadcast_to(e_ref[...], (QT, QT)).astype(F32))
    scale = jnp.where(row == col, power, 0.0).astype(BF)
    x = dot(scale, x_ref[...]).astype(BF)
    o_ref[0:QT] = x[:, 0:128]
    o_ref[QT : 2 * QT] = x[:, 128:256]
    tail = x[:, 256:288].astype(F32)
    o_ref[2 * QT : 360] = jnp.concatenate([tail[40 * j : 40 * j + 40] for j in range(4)], axis=1).astype(BF)


def order_quarters(one, two, after, o_ref):
    del after
    swapped = lax.axis_index("zl") == 1
    o_ref[0] = jnp.where(swapped, one[...], two[...])
    o_ref[1] = jnp.where(swapped, two[...], one[...])


def merge_codes(a_ref, b_ref, c_ref, d_ref, after1, after2, *outs):
    del after1, after2
    pieces = (a_ref, b_ref, c_ref, d_ref)
    for q, o_ref in enumerate(outs):
        for j, ref in enumerate(pieces):
            o_ref[:, 256 * j : 256 * j + 128] = ref[q, 0:QT]
            o_ref[:, 256 * j + 128 : 256 * j + 256] = ref[q, QT : 2 * QT]
        tails = [ref[q, 2 * QT : 360].astype(F32) for ref in pieces]
        groups = [jnp.concatenate([t[:, 32 * j : 32 * j + 32] for t in tails], axis=1) for j in range(4)]
        o_ref[:, 1024:1152] = jnp.concatenate(groups, axis=0).astype(BF)


def own_place():
    c, y, x = lax.axis_index("c"), lax.axis_index("y"), lax.axis_index("x")
    return c, jnp.where(c == 0, y, x), jnp.where(c == 0, x, y)


def arrange_rows(own, ref, w_ref, sem):
    c, first, second = own_place()
    for i in range(4):
        s = lax.rem(second + 4 - ARRIVES[i], 4)
        for j in range(4):
            f = lax.rem(first + 4 - GATHER[j], 4)
            y, x = jnp.where(c == 0, f, s), jnp.where(c == 0, s, f)
            row = lax.rem(y, 2) * UNITS + x * PIECE

            @pl.when((lax.div(y, 2) == c) == own)
            def _():
                for at, to, n in ((0, 256 * j, 256), (256, 1024 + 32 * j, 32)):
                    pltpu.make_async_copy(
                        ref.at[pl.ds(pl.multiple_of(row + at, 32), n)], w_ref.at[pl.ds(i * UNITS + to, n)], sem
                    ).start()

    pltpu.make_async_copy(w_ref.at[: 2 * UNITS], w_ref.at[: 2 * UNITS], sem).wait()


def arrange_own(ref, w_ref, sem):
    arrange_rows(True, ref, w_ref, sem)


def arrange_other(ref, half_ref, w_ref, sem):
    del half_ref
    arrange_rows(False, ref, w_ref, sem)


def stage_own(ref, after, w_ref, sem):
    del after
    copy = pltpu.make_async_copy(ref, w_ref.at[:, : 2 * UNITS], sem)
    copy.start()
    copy.wait()


def stage_other(ref, half_ref, w_ref, sem):
    del half_ref
    copy = pltpu.make_async_copy(ref, w_ref.at[:, 2 * UNITS :], sem)
    copy.start()
    copy.wait()


def scaled(x, most=None):
    most = jnp.full((8, x.shape[1]), jnp.max(jnp.abs(x) if most is None else most))
    power = 13.0 - jnp.ceil(jnp.log(jnp.maximum(most, 1e-30)) * 1.4426950408889634)
    return x * jnp.exp2(power)[:1], power


def project_early(m0, m1, w_ref, o_ref):
    for n in range(0, UNITS, 256):
        to = min(n + 256, UNITS)
        x = jnp.concatenate([m0[...], m1[...]], axis=1)
        o_ref[:, n:to] = dot(x, w_ref[: 2 * UNITS, n:to])


def project_in(m2, m3, w_ref, early_ref, o_ref, send_ref):
    most = jnp.zeros((QT, 128), F32)
    for n in range(0, UNITS, 256):
        to = min(n + 256, UNITS)
        x = jnp.concatenate([m2[...], m3[...]], axis=1)
        part = early_ref[:, n:to] + dot(x, w_ref[2 * UNITS :, n:to])
        o_ref[:, n:to] = part
        for k in range(0, to - n, 128):
            most = jnp.maximum(most, jnp.abs(part[:, k : k + 128]))
    send_ref[0:QT], send_ref[QT:] = scaled(o_ref[...], most)


def project_out(a_ref, w_ref, o0, o1, o2, o3, t_ref, tail_ref):
    for g in range(4):
        for n in range(0, UNITS, 256):
            to = min(n + 256, UNITS)
            part = dot(a_ref[...], w_ref[:, g * UNITS + n : g * UNITS + to])
            t_ref[g, n:to] = part[:128].T
            tail_ref[32 * g : 32 * g + 32, n:to] = part[128:]
    t_ref[4] = tail_ref[...].T
    c, first, _ = own_place()
    for rel, o in zip(STEPS, (o0, o1, o2, o3)):
        f = lax.rem(first + rel, 4)
        for s in range(4):
            at = pl.ds(pl.multiple_of(jnp.where(c == 0, f * 4 + s, s * 4 + f) * CHIP_COLS, 8), CHIP_COLS)
            for p in range(2):
                both = jnp.concatenate([t_ref[2 * p, at], t_ref[2 * p + 1, at]], axis=0)
                o[s, 144 * p : 144 * p + 144] = both.astype(o.dtype)
            o[s, 288:360] = t_ref[4, at].astype(o.dtype)


def add_first(a0, b0, c0, d0, a1, b1, c1, d1, o0, o1, o2, o3):
    _, _, second = own_place()
    for rel, o in zip(STEPS, (o0, o1, o2, o3)):
        s = lax.rem(second + rel, 4)
        total = [
            a[s] + b[s].astype(F32) + c[s].astype(F32) + d[s].astype(F32) for a, b, c, d in ((a0, b0, c0, d0), (a1, b1, c1, d1))
        ]
        o[...] = jnp.concatenate(total, axis=0).astype(o.dtype)


def add_second(a, b, c, d, keep, to_zl, to_c, to_czl):
    total = a[...] + b[...].astype(F32) + c[...].astype(F32) + d[...].astype(F32)
    zl = lax.axis_index("zl")
    tiles = total.reshape(10, CHIP_COLS, 128)
    lane = lax.broadcasted_iota(jnp.int32, (CHIP_COLS, 128), 1)

    def share(crel, z):
        g = 2 * crel + z
        tail = jnp.where(lane < 32, pltpu.roll(tiles[4], (128 - 32 * g) % 128, 1), pltpu.roll(tiles[9], (160 - 32 * g) % 128, 1))
        return tiles[g], tiles[5 + g], tail

    shares = []
    for crel in range(2):
        lo, hi = (jnp.concatenate(share(crel, z), axis=0) for z in range(2))
        shares.append((jnp.where(zl == 0, lo, hi), jnp.where(zl == 0, hi, lo)))
    keep[...] = shares[0][0]
    for ref, value in ((to_zl, shares[0][1]), (to_c, shares[1][0]), (to_czl, shares[1][1])):
        ref[0:216], ref[216:] = scaled(value)


def finish(keep, from_c, from_czl, from_zl, out_ref, o_ref, sem):
    c = lax.axis_index("c")
    whole = [ref[0:216] * jnp.exp2(-ref[216:])[:1] for ref in (from_zl, from_c, from_czl)]
    own, other = keep[...] + whole[0], whole[1] + whole[2]
    cores = jnp.where(c == 0, own, other), jnp.where(c == 0, other, own)
    parts = []
    for q in range(2):
        for v in cores:
            parts += [v[72 * q : 72 * q + 72], v[144:, 32 * q : 32 * q + 32]]
    o_ref[...] = jnp.concatenate(parts, axis=1)
    copy = pltpu.make_async_copy(o_ref, out_ref, sem)
    copy.start()
    copy.wait()


def shape(dims, dtype):
    return jax.ShapeDtypeStruct(dims, dtype)


def in_hbm(x):
    return pltpu.with_memory_space_constraint(x, pltpu.HBM)


def shards(codes, exponents, w_in, w_out):
    zh, zl = lax.axis_index("zh"), lax.axis_index("zl")
    swap = [(0, 1), (1, 0)]
    z = ("zh", "zl")
    w_in_other = lax.ppermute(w_in, "c", swap)
    w_out_other = lax.ppermute(w_out, "c", swap)
    w_in, w_out = in_hbm(w_in), in_hbm(w_out)

    packed = call(
        pack_codes,
        shape((360, 128), BF),
        [ANY] * 2,
        [pltpu.VMEM((QT, PIECE), BF), pltpu.VMEM((1, QT), jnp.int32), pltpu.SemaphoreType.DMA((2,))],
        name="pack_codes",
    )(in_hbm(codes), in_hbm(exponents[None, :]))
    one = lax.ppermute(packed, z, [(0, 1), (3, 2), (2, 0), (1, 3)])
    two = lax.ppermute(packed, z, [(2, 1), (1, 2), (0, 0), (3, 3)])
    dma, half = [pltpu.SemaphoreType.DMA], 4608 * 1152 * 2
    rows = call(arrange_own, pltpu.VMEM((4 * UNITS, UNITS), BF), [ANY], dma, nbytes=half, name="arrange_own")(w_in)
    piece = call(order_quarters, shape((2, 360, 128), BF), [VMEM, VMEM, ANY], name="order_quarters")(one, two, rows)
    around = [lax.ppermute(piece, YX, first_axis(k)) for k in GATHER[1:]]
    rows = call(
        arrange_other, pltpu.VMEM((4 * UNITS, UNITS), BF), [ANY, VMEM], dma, nbytes=half, alias={1: 0}, name="arrange_other"
    )(w_in_other, rows)
    quarter = shape((QT, UNITS), BF)
    merged = call(merge_codes, [quarter] * 2, [VMEM] * 4 + [ANY] * 2, name="merge_codes")(piece, *around, rows, w_out_other)
    around = [[lax.ppermute(m, YX, second_axis(k)) for k in GATHER[1:]] for m in merged]

    preacts, sends = [], []
    for q in range(2):
        cost = dict(flops=QT * 4608 * 1152, nbytes=2304 * 1152 * 2)
        early = call(project_early, shape((QT, UNITS), F32), [VMEM] * 3, name="project_early", **cost)(
            merged[q], around[q][GATHER[1:].index(2)], rows
        )
        near = [v for k, v in zip(GATHER[1:], around[q]) if k != 2]
        outs = [shape((QT, UNITS), F32), shape((QT + 8, UNITS), F32)]
        preact, send = call(project_in, outs, [VMEM] * 4, name="project_in", **cost)(*near, rows, early)
        preacts.append(preact)
        sends.append(send.astype(jnp.float16))
    gots = [lax.ppermute(send, "zh", swap) for send in sends]
    columns = call(stage_own, pltpu.VMEM((UNITS, 4 * UNITS), BF), [ANY] * 2, dma, nbytes=half, name="stage_own")(w_out, rows)
    columns = call(
        stage_other, pltpu.VMEM((UNITS, 4 * UNITS), BF), [ANY, VMEM], dma, nbytes=half, alias={1: 0}, name="stage_other"
    )(w_out_other, columns)

    scattered = []
    for preact, got in zip(preacts, gots):
        other = got[:QT].astype(F32) * jnp.exp2(-got[QT : QT + 1].astype(F32))
        activ = jax.nn.gelu(preact + other, approximate=True).astype(BF)
        part = (4, 360, 128)
        mine, *away = call(
            project_out,
            [shape(part, F32)] + [shape(part, BF)] * 3,
            [VMEM] * 2,
            [pltpu.VMEM((5, UNITS, 128), F32), pltpu.VMEM((128, UNITS), F32)],
            flops=2 * QT * 4608 * 1152,
            nbytes=4608 * 1152 * 2,
            vmem=12,
            name="project_out",
        )(activ, columns)
        scattered += [mine] + [lax.ppermute(v, YX, first_axis(k)) for k, v in zip(STEPS[1:], away)]
    part = (720, 128)
    mine, *away = call(add_first, [shape(part, F32)] + [shape(part, BF)] * 3, [VMEM] * 8, name="add_first")(*scattered)
    around = [lax.ppermute(v, YX, second_axis(k)) for k, v in zip(STEPS[1:], away)]
    away = [shape((224, 128), F32)] * 3
    keep, *away = call(add_second, [shape((216, 128), F32)] + away, [VMEM] * 4, name="add_second")(mine, *around)
    to_zl, to_c, to_czl = (v.astype(jnp.float16) for v in away)
    from_c = lax.ppermute(to_c, "c", swap)
    from_czl = lax.ppermute(to_czl, ("c", "zl"), [(0, 3), (1, 2), (2, 1), (3, 0)])
    from_zl = lax.ppermute(to_zl, "zl", swap)
    got = [v.astype(F32) for v in (from_c, from_czl, from_zl)]
    whole = (CHIP_COLS, 4 * QT)
    scratch = [pltpu.VMEM(whole, F32), pltpu.SemaphoreType.DMA]
    return call(finish, pltpu.HBM(whole, F32), [VMEM] * 4, scratch, out_specs=ANY, name="finish")(keep, *got).T


def solution(mesh):
    split = Mesh(mesh.devices.reshape(2, 2, 2, 4, 4), ("zh", "c", "zl", "y", "x"))
    batch, hidden = ("zh", "c"), ("zl", "y", "x")
    placed = (P(batch, hidden), P(batch), P(batch, hidden), P(hidden, batch))
    return jax.shard_map(shards, mesh=split, in_specs=placed, out_specs=P(None, batch + hidden), check_vma=False)
```
